32 devices in a mesh: grp: 2 (over x), blk: 16 (over z, y, core).
Axes of the slice: x: 2, y: 2, z: 4, core: 2. Of those that a mesh axis runs over, the one named last changes fastest.
Arguments:
- activations: bfloat16 [6144, 14336], P(('grp', 'blk')), parts along dimension 0, may hold values from -6 to 6
- errors: bfloat16 [6144, 4096], P(('grp', 'blk')), parts along dimension 0, may hold values from -6 to 6
- err_factors: bfloat16 [16, 13, 4096], P('blk'), may hold values from -0.09375 to 0.09375
- act_factors: bfloat16 [16, 13, 14336], P('blk'), may hold values from -0.046875 to 0.046875
Outputs:
- scores: float32 [16, 6144], P(None, ('grp', 'blk')), parts along dimension 1
The draws below stay inside these ranges and needn't reach their ends.
There are 2 independent parts, one for each index of `grp`. The reference program is written for one: setup_inputs(seed, part) draws one part's arguments, and reference() takes and returns one part's arrays. A program takes and returns all parts, laid end to end along the dimension named above; an argument that names none is the same for every part. Nothing has to cross between parts.
All inputs are finite; a program needn't handle non-finite values.
Results may differ from the reference program's by a relative error of at most 0.0003.
Values may be sent and summed in bfloat16 or wider, within the bound.
No kernel may reach another device: no remote copies, remote signals or barrier semaphores. Data moves between devices by JAX's collectives and lax.ppermute only.
A program may use at most 192 MiB of HBM per device.

```python
import jax
import jax.numpy as jnp

D = 4096
FF = 14336
RANK = 13
TOKENS = 3072
QUERIES = 16


def level_of(own_key, dims, split, smallest, top_value):
    def one(dim, parts):
        heights = jax.random.uniform(jax.random.fold_in(jax.random.fold_in(own_key, 6), dim), (parts,), jnp.float32, smallest / len(split), top_value / len(split))
        return jnp.repeat(jnp.exp(heights), dims[dim] // parts).reshape((-1,) + (1,) * (len(dims) - dim - 1))

    loudness = one(*split[0])
    for cut in split[1:]:
        loudness = loudness * one(*cut)
    return loudness


def normal_values(own_key, extent, spread, limit, pieces=(), kind=jnp.bfloat16):
    drawn = spread * jax.random.normal(own_key, extent, jnp.float32)
    if pieces:
        drawn = drawn * level_of(own_key, extent, pieces, -0.22, 0.18)
    return jnp.clip(drawn, -limit, limit).astype(kind)


def setup_inputs(seed: int = 0, part: int = 0) -> dict:
    splits = jax.random.split(jax.random.key(seed), 5)
    own_keys = jax.random.split(jax.random.fold_in(splits[4], part), 5)
    return {
        "activations": normal_values(own_keys[0], (TOKENS, FF), 1.0, 6.0, ((0, 16),)),
        "errors": normal_values(own_keys[1], (TOKENS, D), 1.0, 6.0, ((0, 16),)),
        "err_factors": normal_values(splits[2], (QUERIES, RANK, D), D ** -0.5, 0.09375, ((0, 16),)),
        "act_factors": normal_values(splits[3], (QUERIES, RANK, FF), FF ** -0.5, 0.046875, ((0, 16),)),
    }


def reference(activations, errors, err_factors, act_factors):
    err_proj = jnp.dot(errors, err_factors.reshape(QUERIES * RANK, D).T, preferred_element_type=jnp.float32)
    act_proj = jnp.dot(activations, act_factors.reshape(QUERIES * RANK, FF).T, preferred_element_type=jnp.float32)
    products = (err_proj * act_proj).reshape(TOKENS, QUERIES, RANK)
    return jnp.sum(products, axis=2).T
```

```python
import functools

import jax
import jax.numpy as jnp
from jax import lax
from jax.experimental import pallas as pl
from jax.experimental.pallas import tpu as pltpu
from jax.sharding import PartitionSpec as P

AXES = ("grp", "blk")
NT = (((1,), (1,)), ((), ()))
SEGS = 16
ROWS = 16
TILES = 13
STEPS = 8


def project_rows(err_rows, act_rows, err_piece, act_piece):
    err_proj = jnp.einsum("td,qrd->qrt", err_rows, err_piece, preferred_element_type=jnp.float32)
    act_proj = jnp.einsum("tf,qrf->qrt", act_rows, act_piece, preferred_element_type=jnp.float32)
    return (err_proj, act_proj)


def gathered(activations, errors, err_factors, act_factors):
    err_width = errors.shape[1]
    joined = jnp.concatenate((err_factors, act_factors), axis=2)
    piece = lax.all_gather(joined, "blk", axis=0, tiled=True)
    err_proj, act_proj = project_rows(
        errors, activations, piece[:, :, :err_width], piece[:, :, err_width:]
    )
    return jnp.sum(err_proj * act_proj, axis=1)


def place(g):
    tile, row = lax.div(g, ROWS), lax.rem(g, ROWS)
    return jnp.where(row < TILES, g, ROWS * row + tile)


def packed_row(local, half, first):
    return jnp.where(local < half, local + half * first, local - half + half * (1 - first))


def pack_kernel(x_ref, err_ref, act_ref, half_ref, both_ref, runs):
    rank, err_width = err_ref.shape[1], err_ref.shape[2]
    ew, aw = err_width // SEGS, act_ref.shape[2] // SEGS
    runs[...] = jnp.zeros_like(runs)
    for s in range(SEGS):
        runs[s * ROWS : s * ROWS + rank, :ew] = err_ref[0, :, s * ew : (s + 1) * ew]
        runs[s * ROWS : s * ROWS + rank, ew:] = act_ref[0, :, s * aw : (s + 1) * aw]
    rows = both_ref.shape[0]
    shape = (rows, SEGS * ROWS)
    local = lax.broadcasted_iota(jnp.int32, shape, 0)
    source = place(packed_row(local, rows // 2, x_ref[0]))
    pick = (source == lax.broadcasted_iota(jnp.int32, shape, 1)).astype(jnp.bfloat16)
    packed = jnp.dot(pick, runs[...], preferred_element_type=jnp.float32).astype(jnp.bfloat16)
    both_ref[...] = packed
    half_ref[...] = packed[: rows // 2]


def pack(x, err, act):
    rank = err.shape[1]
    width = (err.shape[2] + act.shape[2]) // SEGS
    rows = TILES * ROWS
    vmem = pl.BlockSpec(memory_space=pltpu.VMEM)
    return pl.pallas_call(
        pack_kernel,
        out_shape=(
            jax.ShapeDtypeStruct((rows // 2, width), jnp.bfloat16),
            jax.ShapeDtypeStruct((rows, width), jnp.bfloat16),
        ),
        in_specs=[pl.BlockSpec(memory_space=pltpu.SMEM), vmem, vmem],
        out_specs=(vmem, vmem),
        scratch_shapes=[pltpu.VMEM((SEGS * ROWS, width), jnp.bfloat16)],
        compiler_params=pltpu.CompilerParams(vmem_limit_bytes=16 << 20),
        name="pack",
    )(x, err, act)


def score_kernel(blocks, n_pieces, x_ref, *refs):
    pieces = refs[:n_pieces]
    eo_ref, ao_ref, ep_ref, ap_ref, own_ref, par_ref, we, wa, eo, ao, ep, ap = refs[n_pieces:]
    step = pl.program_id(0)
    ew, aw = we.shape[1] // SEGS, wa.shape[1] // SEGS

    @pl.when(step == 0)
    def _():
        half = TILES * ROWS // 2
        x = x_ref[0]
        for b, parts in enumerate(blocks):
            total = None
            for i, other in parts:
                rows = pieces[i].shape[0]
                shape = (SEGS * ROWS, rows)
                out = lax.broadcasted_iota(jnp.int32, shape, 0)
                local = lax.broadcasted_iota(jnp.int32, shape, 1)
                source = place(packed_row(local, half, 1 - x if other else x))
                pick = (source == out).astype(jnp.bfloat16)
                term = jnp.dot(pick, pieces[i][...], preferred_element_type=jnp.float32)
                total = term if total is None else total + term
            total = total.astype(jnp.bfloat16)
            for s in range(SEGS):
                run = total[s * ROWS : (s + 1) * ROWS]
                we[b * ROWS : (b + 1) * ROWS, s * ew : (s + 1) * ew] = run[:, :ew]
                wa[b * ROWS : (b + 1) * ROWS, s * aw : (s + 1) * aw] = run[:, ew:]
        for acc in (eo, ao, ep, ap):
            acc[...] = jnp.zeros_like(acc)

    ec, ac = eo_ref.shape[1], ao_ref.shape[1]
    wec = we[:, pl.ds(pl.multiple_of(step * ec, ec), ec)]
    wac = wa[:, pl.ds(pl.multiple_of(step * ac, ac), ac)]
    for acc, w, t in ((eo, wec, eo_ref), (ep, wec, ep_ref), (ao, wac, ao_ref), (ap, wac, ap_ref)):
        acc[...] += lax.dot_general(w, t[...], NT, preferred_element_type=jnp.float32)

    @pl.when(step == STEPS - 1)
    def _():
        for e, a, o in ((eo, ao, own_ref), (ep, ap, par_ref)):
            prod = e[...] * a[...]
            for b in range(len(blocks)):
                o[b : b + 1, :] = jnp.sum(
                    prod[b * ROWS : (b + 1) * ROWS], axis=0, keepdims=True
                )


def score(x, pieces, blocks, tokens):
    errs, acts = tokens[0].shape[1], tokens[1].shape[1]
    t, nb = tokens[0].shape[0], len(blocks)
    ew, aw = errs // STEPS, acts // STEPS
    whole = lambda a: pl.BlockSpec(a.shape, lambda i: (0, 0))
    cut = lambda w: pl.BlockSpec((t, w), lambda i: (0, i))
    acc = pltpu.VMEM((nb * ROWS, t), jnp.float32)
    out = jax.ShapeDtypeStruct((nb, t), jnp.float32)
    return pl.pallas_call(
        functools.partial(score_kernel, blocks, len(pieces)),
        grid=(STEPS,),
        out_shape=(out, out),
        in_specs=[pl.BlockSpec(memory_space=pltpu.SMEM)]
        + [whole(p) for p in pieces]
        + [cut(ew), cut(aw), cut(ew), cut(aw)],
        out_specs=(whole(out), whole(out)),
        scratch_shapes=[
            pltpu.VMEM((nb * ROWS, errs), jnp.bfloat16),
            pltpu.VMEM((nb * ROWS, acts), jnp.bfloat16),
            acc, acc, acc, acc,
        ],
        compiler_params=pltpu.CompilerParams(vmem_limit_bytes=40 << 20),
        cost_estimate=pl.CostEstimate(
            flops=2 * nb * ROWS * 2 * t * (errs + acts),
            bytes_accessed=4 * t * (errs + acts),
            transcendentals=0,
        ),
        name="score",
    )(x, *pieces, *tokens)


def place_kernel(me_ref, *refs):
    out_ref = refs[-1]
    me = me_ref[0]
    row = 0
    for own, par in zip(refs[:-1:2], refs[1:-1:2]):
        for b in range(own.shape[0]):
            q = jnp.bitwise_xor(me, 2 * row)
            out_ref[pl.ds(q, 1), :] = own[b : b + 1, :]
            out_ref[pl.ds(jnp.bitwise_xor(q, 1), 1), :] = par[b : b + 1, :]
            row += 1


def finish(me, rows, queries, t):
    vmem = pl.BlockSpec(memory_space=pltpu.VMEM)
    return pl.pallas_call(
        place_kernel,
        out_shape=jax.ShapeDtypeStruct((queries, t), jnp.float32),
        in_specs=[pl.BlockSpec(memory_space=pltpu.SMEM)] + [vmem] * len(rows),
        out_specs=vmem,
        name="place",
    )(me, *rows)


def pairs(n_grp, n_blk, flip_grp, flip_blk):
    return [
        (g * n_blk + b, (g ^ flip_grp) * n_blk + (b ^ flip_blk))
        for g in range(n_grp)
        for b in range(n_blk)
    ]


def permuted(n_grp, n_blk, activations, errors, err_factors, act_factors):
    swap = lambda a, gx, bx: lax.ppermute(a, AXES, pairs(n_grp, n_blk, gx, bx))
    over_x = lambda a: swap(a, 1, 0)
    over_y = lambda a: swap(a, 0, 2)
    over_z = lambda a, k: swap(a, 0, 4 * k)
    mate = lambda a: swap(a, 0, 1)
    x = lax.axis_index("grp").astype(jnp.int32).reshape(1)
    me = lax.axis_index("blk").astype(jnp.int32).reshape(1)

    half, both = pack(x, err_factors, act_factors)
    z2, z3 = over_z(half, 2), over_z(half, 3)
    z1 = over_z(both, 1)
    y0 = over_y(both)
    tokens = (errors, activations, mate(errors), mate(activations))
    y2, xa2 = over_y(z2), over_x(z2)
    xb2 = over_x(y2)
    y3, xa3 = over_y(z3), over_x(z3)
    y1 = over_y(z1)
    xb3 = over_x(y3)

    full = lambda i: ((i, False),)
    split = lambda i: ((i, False), (i + 1, True))
    o0, p0 = score(x, (both, y0, z1, y1), tuple(full(i) for i in range(4)), tokens)
    o2, p2 = score(x, (z2, xa2, y2, xb2), (split(0), split(2)), tokens)
    o3, p3 = score(x, (z3, xa3, y3, xb3), (split(0), split(2)), tokens)
    rows = (o0, mate(p0), o2, mate(p2), o3, mate(p3))
    return finish(me, rows, n_blk, errors.shape[0])


def solution(mesh):
    in_specs = (
        P(("grp", "blk"), None),
        P(("grp", "blk"), None),
        P("blk", None, None),
        P("blk", None, None),
    )
    out_specs = P(None, ("grp", "blk"))
    n_grp, n_blk = mesh.shape["grp"], mesh.shape["blk"]
    body = gathered
    if (n_grp, n_blk) == (2, 16):
        body = functools.partial(permuted, n_grp, n_blk)
    return jax.shard_map(body, mesh=mesh, in_specs=in_specs, out_specs=out_specs, check_vma=False)
```

```python
import functools

import jax
import jax.numpy as jnp
from jax import lax
from jax.experimental import pallas as pl
from jax.experimental.pallas import tpu as pltpu
from jax.sharding import PartitionSpec as P

AXES = ("grp", "blk")
NT = (((1,), (1,)), ((), ()))
RANK = 13
SEGS = 16
ROWS = 16
CUTS = 4


def project_rows(err_rows, act_rows, err_piece, act_piece):
    err_proj = jnp.einsum("td,qrd->qrt", err_rows, err_piece, preferred_element_type=jnp.float32)
    act_proj = jnp.einsum("tf,qrf->qrt", act_rows, act_piece, preferred_element_type=jnp.float32)
    return (err_proj, act_proj)


def gathered(activations, errors, err_factors, act_factors):
    err_width = errors.shape[1]
    joined = jnp.concatenate((err_factors, act_factors), axis=2)
    piece = lax.all_gather(joined, "blk", axis=0, tiled=True)
    err_proj, act_proj = project_rows(
        errors, activations, piece[:, :, :err_width], piece[:, :, err_width:]
    )
    return jnp.sum(err_proj * act_proj, axis=1)


def picks(shape, stacked_dim, offset):
    stacked = lax.broadcasted_iota(jnp.int32, shape, stacked_dim)
    packed = lax.broadcasted_iota(jnp.int32, shape, 1 - stacked_dim) - offset
    m, r = stacked >> 4, stacked & 15
    return ((r < RANK) & (packed == RANK * m + r)).astype(jnp.bfloat16)


def pack_kernel(first, x_ref, err_ref, act_ref, out_ref, runs):
    ew, aw = err_ref.shape[2] // SEGS, act_ref.shape[2] // SEGS
    n = SEGS // 2
    rows = n * RANK
    runs[...] = jnp.zeros_like(runs)
    for s in range(SEGS):
        runs[s // n, s % n * ROWS : s % n * ROWS + RANK, :ew] = err_ref[0, :, s * ew : (s + 1) * ew]
        runs[s // n, s % n * ROWS : s % n * ROWS + RANK, ew:] = act_ref[0, :, s * aw : (s + 1) * aw]
    x = x_ref[0]
    total = None
    for i, h in enumerate((x,) if first else (x, 1 - x)):
        pick = picks((out_ref.shape[0], n * ROWS), 1, i * rows)
        term = jnp.dot(pick, runs[h], preferred_element_type=jnp.float32)
        total = term if total is None else total + term
    out_ref[...] = total.astype(jnp.bfloat16)


def pack(x, err, act, first):
    width = (err.shape[2] + act.shape[2]) // SEGS
    n = SEGS // 2
    vmem = pl.BlockSpec(memory_space=pltpu.VMEM)
    return pl.pallas_call(
        functools.partial(pack_kernel, first),
        out_shape=jax.ShapeDtypeStruct(((1 if first else 2) * n * RANK, width), jnp.bfloat16),
        in_specs=[pl.BlockSpec(memory_space=pltpu.SMEM), vmem, vmem],
        out_specs=vmem,
        scratch_shapes=[pltpu.VMEM((2, n * ROWS, width), jnp.bfloat16)],
        compiler_params=pltpu.CompilerParams(vmem_limit_bytes=16 << 20),
        cost_estimate=None if first else weight(20),
        name="pack",
    )(x, err, act)


def weight(us):
    return pl.CostEstimate(flops=int(us * 1e9), bytes_accessed=int(us * 3e6), transcendentals=0)


def score_kernel(jobs, n_pieces, n_in, last, x_ref, *refs):
    pieces, refs = refs[:n_pieces], refs[n_pieces:]
    (eo_ref, ao_ref, ep_ref, ap_ref), refs = refs[:4], refs[4:]
    accs_in, refs = refs[:n_in], refs[n_in:]
    outs, (we, wa) = refs[:-2], refs[-2:]
    n = SEGS // 2
    ew, aw = we.shape[1] // n, wa.shape[1] // n
    x = x_ref[0]
    sums = [a[...] for a in accs_in] if n_in else [None] * 4
    for other, parts in jobs:
        for b, (i, offset) in enumerate(parts):
            pick = picks((n * ROWS, pieces[i].shape[0]), 0, offset)
            run = jnp.dot(pick, pieces[i][...], preferred_element_type=jnp.float32)
            run = run.astype(jnp.bfloat16)
            for s in range(n):
                own = run[s * ROWS : (s + 1) * ROWS]
                we[b * ROWS : (b + 1) * ROWS, s * ew : (s + 1) * ew] = own[:, :ew]
                wa[b * ROWS : (b + 1) * ROWS, s * aw : (s + 1) * aw] = own[:, ew:]
        half = 1 - x if other else x
        for j, (w, t_ref) in enumerate(((we, eo_ref), (wa, ao_ref), (we, ep_ref), (wa, ap_ref))):
            width = w.shape[1]
            cut = width // CUTS
            for i in range(CUTS):
                at = pl.ds(pl.multiple_of(half * width + i * cut, cut), cut)
                term = lax.dot_general(
                    w[:, i * cut : (i + 1) * cut], t_ref[:, at], NT,
                    preferred_element_type=jnp.float32,
                )
                sums[j] = term if sums[j] is None else sums[j] + term
    if not last:
        for o, v in zip(outs, sums):
            o[...] = v
        return
    for o, e, a in zip(outs, sums[::2], sums[1::2]):
        prod = e * a
        for b in range(o.shape[0]):
            o[b : b + 1, :] = jnp.sum(prod[b * ROWS : (b + 1) * ROWS], axis=0, keepdims=True)


def score(x, pieces, jobs, tokens, accs=(), last=True):
    errs, acts = tokens[0].shape[1], tokens[1].shape[1]
    t, nb = tokens[0].shape[0], len(jobs[0][1])
    vmem = pl.BlockSpec(memory_space=pltpu.VMEM)
    if last:
        outs = (jax.ShapeDtypeStruct((nb, t), jnp.float32),) * 2
    else:
        outs = (jax.ShapeDtypeStruct((nb * ROWS, t), jnp.float32),) * 4
    return pl.pallas_call(
        functools.partial(score_kernel, jobs, len(pieces), len(accs), last),
        out_shape=outs,
        in_specs=[pl.BlockSpec(memory_space=pltpu.SMEM)]
        + [vmem] * (len(pieces) + 4 + len(accs)),
        out_specs=(vmem,) * len(outs),
        scratch_shapes=[
            pltpu.VMEM((nb * ROWS, errs // 2), jnp.bfloat16),
            pltpu.VMEM((nb * ROWS, acts // 2), jnp.bfloat16),
        ],
        compiler_params=pltpu.CompilerParams(vmem_limit_bytes=32 << 20),
        cost_estimate=weight(30),
        name="score",
    )(x, *pieces, *tokens, *accs)


def place_kernel(me_ref, *refs):
    out_ref = refs[-1]
    me = me_ref[0]
    row = 0
    for own, par in zip(refs[:-1:2], refs[1:-1:2]):
        for b in range(own.shape[0]):
            q = jnp.bitwise_xor(me, 2 * row)
            out_ref[pl.ds(q, 1), :] = own[b : b + 1, :]
            out_ref[pl.ds(jnp.bitwise_xor(q, 1), 1), :] = par[b : b + 1, :]
            row += 1


def finish(me, rows, queries, t):
    vmem = pl.BlockSpec(memory_space=pltpu.VMEM)
    return pl.pallas_call(
        place_kernel,
        out_shape=jax.ShapeDtypeStruct((queries, t), jnp.float32),
        in_specs=[pl.BlockSpec(memory_space=pltpu.SMEM)] + [vmem] * len(rows),
        out_specs=vmem,
        name="place",
    )(me, *rows)


def pairs(n_grp, n_blk, flip_grp, flip_blk):
    return [
        (g * n_blk + b, (g ^ flip_grp) * n_blk + (b ^ flip_blk))
        for g in range(n_grp)
        for b in range(n_blk)
    ]


def after(*arrays):
    return lax.optimization_barrier(arrays)


def permuted(n_grp, n_blk, activations, errors, err_factors, act_factors):
    swap = lambda a, gx, bx: lax.ppermute(a, AXES, pairs(n_grp, n_blk, gx, bx))
    over_x = lambda a: swap(a, 1, 0)
    over_y = lambda a: swap(a, 0, 2)
    over_z = lambda a, k: swap(a, 0, 4 * k)
    mate = lambda a: swap(a, 0, 1)
    x = lax.axis_index("grp").astype(jnp.int32).reshape(1)
    me = lax.axis_index("blk").astype(jnp.int32).reshape(1)

    half = pack(x, err_factors, act_factors, True)
    mate_acts = mate(activations)
    mate_errs = mate(errors)
    z3 = over_z(half, 3)
    x_late, half = after(x, half)
    both = pack(x_late, err_factors, act_factors, False)
    y0, z1 = over_y(both), over_z(both, 1)
    y3, xa3 = over_y(z3), over_x(z3)
    z2 = over_z(z3, 1)
    n = half.shape[0]
    y1m = over_y(z1[:n])

    tokens = (errors, activations, mate_errs, mate_acts)
    y0, z3 = after(y0, z3)
    o0, p0 = score(
        x, (both, y0), ((False, ((0, 0), (1, 0))), (True, ((0, n), (1, n)))), tokens
    )
    z2, y3, z1, o0 = after(z2, y3, z1, o0)
    xb3 = over_x(y3)
    y2, xa2 = over_y(z2), over_x(z2)
    y1o = over_y(z1[n:])
    xb2 = over_x(y2)

    z2, xa3, xa2, xb3 = after(z2, xa3, xa2, xb3)
    five = tuple((i, 0) for i in range(1, 6))
    accs = score(x, (z1, y1m, z2, y2, z3, y3), ((False, ((0, 0),) + five),), tokens, last=False)
    o1, p1 = score(
        x, (z1, y1o, xa2, xb2, xa3, xb3), ((True, ((0, n),) + five),), tokens, accs
    )
    rows = (o0, mate(p0), o1, mate(p1))
    return finish(me, rows, n_blk, errors.shape[0])


def solution(mesh):
    in_specs = (
        P(("grp", "blk"), None),
        P(("grp", "blk"), None),
        P("blk", None, None),
        P("blk", None, None),
    )
    out_specs = P(None, ("grp", "blk"))
    n_grp, n_blk = mesh.shape["grp"], mesh.shape["blk"]
    body = gathered
    if (n_grp, n_blk) == (2, 16):
        body = functools.partial(permuted, n_grp, n_blk)
    return jax.shard_map(body, mesh=mesh, in_specs=in_specs, out_specs=out_specs, check_vma=False)
```

```python
import functools

import jax
import jax.numpy as jnp
from jax import lax
from jax.experimental import pallas as pl
from jax.experimental.pallas import tpu as pltpu
from jax.sharding import PartitionSpec as P

AXES = ("grp", "blk")
NT = (((1,), (1,)), ((), ()))
RANK = 13
SEGS = 16
ROWS = 16
CUTS = (1, 4)
AHEAD = 10
LIMIT = 16 << 20
TICK = 8
PACK = 30


def project_rows(err_rows, act_rows, err_piece, act_piece):
    err_proj = jnp.einsum("td,qrd->qrt", err_rows, err_piece, preferred_element_type=jnp.float32)
    act_proj = jnp.einsum("tf,qrf->qrt", act_rows, act_piece, preferred_element_type=jnp.float32)
    return (err_proj, act_proj)


def gathered(activations, errors, err_factors, act_factors):
    err_width = errors.shape[1]
    joined = jnp.concatenate((err_factors, act_factors), axis=2)
    piece = lax.all_gather(joined, "blk", axis=0, tiled=True)
    err_proj, act_proj = project_rows(
        errors, activations, piece[:, :, :err_width], piece[:, :, err_width:]
    )
    return jnp.sum(err_proj * act_proj, axis=1)


def picks(shape, stacked_dim):
    stacked = lax.broadcasted_iota(jnp.int32, shape, stacked_dim)
    packed = lax.broadcasted_iota(jnp.int32, shape, 1 - stacked_dim)
    m, r = stacked >> 4, stacked & 15
    return ((r < RANK) & (packed == RANK * m + r)).astype(jnp.bfloat16)


def pack_kernel(x_ref, err_hbm, act_hbm, half_ref, runs, err_ref, act_ref, sems):
    ew, aw = err_ref.shape[2] // SEGS, act_ref.shape[2] // SEGS
    n = SEGS // 2
    copies = [
        pltpu.make_async_copy(err_hbm, err_ref, sems.at[0]),
        pltpu.make_async_copy(act_hbm, act_ref, sems.at[1]),
    ]
    for copy in copies:
        copy.start()
    runs[...] = jnp.zeros_like(runs)
    for copy in copies:
        copy.wait()
    for s in range(SEGS):
        runs[s // n, s % n * ROWS : s % n * ROWS + RANK, :ew] = err_ref[0, :, s * ew : (s + 1) * ew]
        runs[s // n, s % n * ROWS : s % n * ROWS + RANK, ew:] = act_ref[0, :, s * aw : (s + 1) * aw]
    pick = picks((half_ref.shape[0], n * ROWS), 1)
    half = jnp.dot(pick, runs[x_ref[0]], preferred_element_type=jnp.float32)
    half_ref[...] = half.astype(jnp.bfloat16)


def pack(x, err, act):
    width = (err.shape[2] + act.shape[2]) // SEGS
    n = SEGS // 2
    vmem, hbm = pl.BlockSpec(memory_space=pltpu.VMEM), pl.BlockSpec(memory_space=pltpu.HBM)
    return pl.pallas_call(
        pack_kernel,
        out_shape=(
            jax.ShapeDtypeStruct((n * RANK, width), jnp.bfloat16),
            jax.ShapeDtypeStruct((2, n * ROWS, width), jnp.bfloat16),
        ),
        in_specs=[pl.BlockSpec(memory_space=pltpu.SMEM), hbm, hbm],
        out_specs=(vmem, vmem),
        scratch_shapes=[
            pltpu.VMEM(err.shape, err.dtype),
            pltpu.VMEM(act.shape, act.dtype),
            pltpu.SemaphoreType.DMA((2,)),
        ],
        compiler_params=pltpu.CompilerParams(vmem_limit_bytes=LIMIT),
        name="pack",
    )(x, err, act)


def again_kernel(x_ref, runs, half_ref, rest_ref):
    n = SEGS // 2
    pick = picks((half_ref.shape[0], n * ROWS), 1)
    for h, out_ref in ((x_ref[0], half_ref), (1 - x_ref[0], rest_ref)):
        half = jnp.dot(pick, runs[h], preferred_element_type=jnp.float32)
        out_ref[...] = half.astype(jnp.bfloat16)


def pack_again(x, runs):
    vmem = pl.BlockSpec(memory_space=pltpu.VMEM)
    out = jax.ShapeDtypeStruct((SEGS // 2 * RANK, runs.shape[2]), jnp.bfloat16)
    return pl.pallas_call(
        again_kernel,
        out_shape=(out, out),
        in_specs=[pl.BlockSpec(memory_space=pltpu.SMEM), vmem],
        out_specs=(vmem, vmem),
        compiler_params=pltpu.CompilerParams(vmem_limit_bytes=LIMIT),
        cost_estimate=weight(PACK),
        name="pack_again",
    )(x, runs)


def weight(us):
    return pl.CostEstimate(flops=int(us * 1e9), bytes_accessed=int(us * 3e6), transcendentals=0)


def unpack(piece, out_ref, at, ew):
    n = SEGS // 2
    aw = piece.shape[1] - ew
    pick = picks((n * ROWS, piece.shape[0]), 0)
    runs = jnp.dot(pick, piece[...], preferred_element_type=jnp.float32).astype(jnp.bfloat16)
    for s in range(n):
        run = runs[s * ROWS : (s + 1) * ROWS]
        out_ref[at : at + ROWS, s * ew : (s + 1) * ew] = run[:, :ew]
        out_ref[at : at + ROWS, n * ew + s * aw : n * ew + (s + 1) * aw] = run[:, ew:]


def gate_kernel(*refs):
    pass


def gate(*arrays):
    hbm = pl.BlockSpec(memory_space=pl.ANY)
    return pl.pallas_call(
        gate_kernel,
        out_shape=tuple(jax.ShapeDtypeStruct(a.shape, a.dtype) for a in arrays),
        in_specs=[hbm] * len(arrays),
        out_specs=(hbm,) * len(arrays),
        input_output_aliases={i: i for i in range(len(arrays))},
        compiler_params=pltpu.CompilerParams(vmem_limit_bytes=1 << 20),
        cost_estimate=weight(TICK),
        name="gate",
    )(*arrays)


def fetch(half, tokens, buffers, sems):
    jobs = []
    for j in range(4):
        width, side = buffers[j].shape[1], j % 2
        start = side * buffers[0].shape[1]
        cut = width // CUTS[side]
        for i in range(CUTS[side]):
            at = pl.ds(pl.multiple_of(half * width + i * cut, cut), cut)
            copy = pltpu.make_async_copy(
                tokens[j].at[:, at], buffers[j].at[:, pl.ds(i * cut, cut)], sems.at[len(jobs)]
            )
            jobs.append((copy, j, i * cut, start + i * cut, cut))
    for job in jobs[:AHEAD]:
        job[0].start()
    return jobs


def project(rows, jobs, buffers):
    sums = [None] * 4
    for i, (copy, j, first, start, cut) in enumerate(jobs):
        copy.wait()
        if i + AHEAD < len(jobs):
            jobs[i + AHEAD][0].start()
        term = lax.dot_general(
            rows[:, start : start + cut], buffers[j][:, first : first + cut], NT,
            preferred_element_type=jnp.float32,
        )
        sums[j] = term if sums[j] is None else sums[j] + term
    return sums


def half_scratch(tokens):
    return [pltpu.VMEM((a.shape[0], a.shape[1] // 2), a.dtype) for a in tokens] + [
        pltpu.SemaphoreType.DMA((2 * sum(CUTS),))
    ]


def unpack_kernel(now, later, ew, *refs):
    pieces, (now_ref, later_ref) = refs[:-2], refs[-2:]
    for out_ref, parts in ((now_ref, now), (later_ref, later)):
        for i, p in enumerate(parts):
            unpack(pieces[p], out_ref, i * ROWS, ew)


def unpacked(pieces, now, later, ew):
    vmem = pl.BlockSpec(memory_space=pltpu.VMEM)
    width = SEGS // 2 * pieces[0].shape[1]
    return pl.pallas_call(
        functools.partial(unpack_kernel, now, later, ew),
        out_shape=tuple(
            jax.ShapeDtypeStruct((len(p) * ROWS, width), jnp.bfloat16) for p in (now, later)
        ),
        in_specs=[vmem] * len(pieces),
        out_specs=(vmem, vmem),
        compiler_params=pltpu.CompilerParams(vmem_limit_bytes=LIMIT),
        cost_estimate=weight(TICK),
        name="unpacked",
    )(*pieces)


def first_kernel(now, later, n_pieces, x_ref, rows_ref, *refs):
    pieces, refs = refs[:n_pieces], refs[n_pieces:]
    tokens, accs, (later_ref, rows, *buffers, sems) = refs[:4], refs[4:8], refs[8:]
    jobs = fetch(x_ref[0], tokens, buffers, sems)
    ew, n = tokens[0].shape[1] // SEGS, rows_ref.shape[0]
    rows[:n] = rows_ref[...]
    for i, p in enumerate(now):
        unpack(pieces[p], rows, n + i * ROWS, ew)
    for acc, v in zip(accs, project(rows, jobs, buffers)):
        acc[...] = v
    for i, p in enumerate(later):
        unpack(pieces[p], later_ref, i * ROWS, ew)


def first_half(x, rows, pieces, now, later, tokens):
    vmem, hbm = pl.BlockSpec(memory_space=pltpu.VMEM), pl.BlockSpec(memory_space=pltpu.HBM)
    n, width = rows.shape[0] + len(now) * ROWS, rows.shape[1]
    acc = jax.ShapeDtypeStruct((n, tokens[0].shape[0]), jnp.float32)
    return pl.pallas_call(
        functools.partial(first_kernel, now, later, len(pieces)),
        out_shape=(acc,) * 4
        + (jax.ShapeDtypeStruct((len(later) * ROWS, width), jnp.bfloat16),),
        in_specs=[pl.BlockSpec(memory_space=pltpu.SMEM)] + [vmem] * (len(pieces) + 1) + [hbm] * 4,
        out_specs=(vmem,) * 5,
        scratch_shapes=[pltpu.VMEM((n, width), jnp.bfloat16)] + half_scratch(tokens),
        compiler_params=pltpu.CompilerParams(vmem_limit_bytes=LIMIT),
        cost_estimate=weight(12),
        name="first_half",
    )(x, rows, *pieces, *tokens)


def second_kernel(order, n_pieces, x_ref, me_ref, rows_a, rows_b, *refs):
    pieces, refs = refs[:n_pieces], refs[n_pieces:]
    tokens, accs = refs[:4], refs[4:8]
    own_ref, mate_ref, rows, *buffers, sems = refs[8:]
    jobs = fetch(1 - x_ref[0], tokens, buffers, sems)
    n, m = rows_a.shape[0], rows_a.shape[0] + rows_b.shape[0]
    rows[:n], rows[n:m] = rows_a[...], rows_b[...]
    for i, piece in enumerate(pieces):
        unpack(piece, rows, m + i * ROWS, tokens[0].shape[1] // SEGS)
    me = me_ref[0]
    sums = [v + acc[...] for v, acc in zip(project(rows, jobs, buffers), accs)]
    for j, out_ref in enumerate((own_ref, mate_ref)):
        prod = sums[2 * j] * sums[2 * j + 1]
        out_ref[...] = jnp.zeros_like(out_ref)
        for b, flip in enumerate(order):
            row = jnp.sum(prod[b * ROWS : (b + 1) * ROWS], axis=0, keepdims=True)
            out_ref[pl.ds(jnp.bitwise_xor(me, flip), 1), :] = row


def second_half(x, me, order, rows_a, rows_b, pieces, tokens, accs):
    vmem, smem = pl.BlockSpec(memory_space=pltpu.VMEM), pl.BlockSpec(memory_space=pltpu.SMEM)
    hbm = pl.BlockSpec(memory_space=pltpu.HBM)
    out = jax.ShapeDtypeStruct((2 * len(order), tokens[0].shape[0]), jnp.float32)
    return pl.pallas_call(
        functools.partial(second_kernel, order, len(pieces)),
        out_shape=(out, out),
        in_specs=[smem, smem] + [vmem] * (2 + len(pieces)) + [hbm] * 4 + [vmem] * 4,
        out_specs=(vmem, vmem),
        scratch_shapes=[pltpu.VMEM((len(order) * ROWS, rows_a.shape[1]), jnp.bfloat16)]
        + half_scratch(tokens),
        compiler_params=pltpu.CompilerParams(vmem_limit_bytes=LIMIT),
        cost_estimate=weight(10),
        name="second_half",
    )(x, me, rows_a, rows_b, *pieces, *tokens, *accs)


def pairs(n_grp, n_blk, flip_grp, flip_blk):
    return [
        (g * n_blk + b, (g ^ flip_grp) * n_blk + (b ^ flip_blk))
        for g in range(n_grp)
        for b in range(n_blk)
    ]


def in_hbm(a):
    return pltpu.with_memory_space_constraint(a, pltpu.HBM)


def permuted(n_grp, n_blk, activations, errors, err_factors, act_factors):
    swap = lambda a, gx, bx: lax.ppermute(a, AXES, pairs(n_grp, n_blk, gx, bx))
    over_x = lambda a: swap(a, 1, 0)
    over_y = lambda a: swap(a, 0, 2)
    over_z = lambda a, k: swap(a, 0, 4 * k)
    mate = lambda a: swap(a, 0, 1)
    x = lax.axis_index("grp").astype(jnp.int32).reshape(1)
    me = lax.axis_index("blk").astype(jnp.int32).reshape(1)

    mate_acts, mate_errs = mate(activations), mate(errors)
    half, runs = pack(x, in_hbm(err_factors), in_hbm(act_factors))
    z3 = over_z(half, 3)
    half, rest = pack_again(x, runs)
    y0, z1, y0r = over_y(half), over_z(half, 1), over_y(rest)
    z3, z1, y0, y0r, rest, mate_acts = gate(z3, z1, y0, y0r, rest, mate_acts)
    z2, y3, xa3 = over_z(z3, 1), over_y(z3), over_x(z3)
    y1, y1r = over_y(z1), over_z(y0r, 1)
    z2, y3, xa3, rest = gate(z2, y3, xa3, rest)
    y2, xa2, xb3 = over_y(z2), over_x(z2), over_x(y3)
    z1r = over_z(rest, 1)
    mine, others = unpacked(
        (half, y0, z3, z1, y1, z2, y3, rest, y0r, xa3), tuple(range(7)), (7, 8, 9),
        errors.shape[1] // SEGS,
    )
    xb2 = over_x(y2)

    tokens = tuple(in_hbm(a) for a in (errors, activations, mate_errs, mate_acts))
    *accs, late = first_half(x, mine, (y2, z1r, y1r), (0,), (1, 2), tokens)
    order = (0, 2, 12, 4, 6, 8, 14, 10)
    own, mates = second_half(x, me, order, others, late, (xa2, xb3, xb2), tokens, accs)
    return own + mate(mates)


def solution(mesh):
    in_specs = (
        P(("grp", "blk"), None),
        P(("grp", "blk"), None),
        P("blk", None, None),
        P("blk", None, None),
    )
    out_specs = P(None, ("grp", "blk"))
    n_grp, n_blk = mesh.shape["grp"], mesh.shape["blk"]
    body = gathered
    if (n_grp, n_blk) == (2, 16):
        body = functools.partial(permuted, n_grp, n_blk)
    return jax.shard_map(body, mesh=mesh, in_specs=in_specs, out_specs=out_specs, check_vma=False)
```

```python
import functools

import jax
import jax.numpy as jnp
from jax import lax
from jax.experimental import pallas as pl
from jax.experimental.pallas import tpu as pltpu
from jax.sharding import PartitionSpec as P

AXES = ("grp", "blk")
NT = (((1,), (1,)), ((), ()))
RANK = 13
SEGS = 16
ROWS = 16
CUTS = (1, 4)
LIMIT = 16 << 20
TICK = 8
PACK = 30


def project_rows(err_rows, act_rows, err_piece, act_piece):
    err_proj = jnp.einsum("td,qrd->qrt", err_rows, err_piece, preferred_element_type=jnp.float32)
    act_proj = jnp.einsum("tf,qrf->qrt", act_rows, act_piece, preferred_element_type=jnp.float32)
    return (err_proj, act_proj)


def gathered(activations, errors, err_factors, act_factors):
    err_width = errors.shape[1]
    joined = jnp.concatenate((err_factors, act_factors), axis=2)
    piece = lax.all_gather(joined, "blk", axis=0, tiled=True)
    err_proj, act_proj = project_rows(
        errors, activations, piece[:, :, :err_width], piece[:, :, err_width:]
    )
    return jnp.sum(err_proj * act_proj, axis=1)


def picks(shape, stacked_dim):
    stacked = lax.broadcasted_iota(jnp.int32, shape, stacked_dim)
    packed = lax.broadcasted_iota(jnp.int32, shape, 1 - stacked_dim)
    m, r = stacked >> 4, stacked & 15
    return ((r < RANK) & (packed == RANK * m + r)).astype(jnp.bfloat16)


def pack_kernel(x_ref, err_hbm, act_hbm, half_ref, runs, err_ref, act_ref, sems):
    ew, aw = err_ref.shape[2] // SEGS, act_ref.shape[2] // SEGS
    n = SEGS // 2
    copies = [
        pltpu.make_async_copy(err_hbm, err_ref, sems.at[0]),
        pltpu.make_async_copy(act_hbm, act_ref, sems.at[1]),
    ]
    for copy in copies:
        copy.start()
    runs[...] = jnp.zeros_like(runs)
    for copy in copies:
        copy.wait()
    for s in range(SEGS):
        runs[s // n, s % n * ROWS : s % n * ROWS + RANK, :ew] = err_ref[0, :, s * ew : (s + 1) * ew]
        runs[s // n, s % n * ROWS : s % n * ROWS + RANK, ew:] = act_ref[0, :, s * aw : (s + 1) * aw]
    pick = picks((half_ref.shape[0], n * ROWS), 1)
    half = jnp.dot(pick, runs[x_ref[0]], preferred_element_type=jnp.float32)
    half_ref[...] = half.astype(jnp.bfloat16)


def pack(x, err, act):
    width = (err.shape[2] + act.shape[2]) // SEGS
    n = SEGS // 2
    vmem, hbm = pl.BlockSpec(memory_space=pltpu.VMEM), pl.BlockSpec(memory_space=pltpu.HBM)
    return pl.pallas_call(
        pack_kernel,
        out_shape=(
            jax.ShapeDtypeStruct((n * RANK, width), jnp.bfloat16),
            jax.ShapeDtypeStruct((2, n * ROWS, width), jnp.bfloat16),
        ),
        in_specs=[pl.BlockSpec(memory_space=pltpu.SMEM), hbm, hbm],
        out_specs=(vmem, vmem),
        scratch_shapes=[
            pltpu.VMEM(err.shape, err.dtype),
            pltpu.VMEM(act.shape, act.dtype),
            pltpu.SemaphoreType.DMA((2,)),
        ],
        compiler_params=pltpu.CompilerParams(vmem_limit_bytes=LIMIT),
        name="pack",
    )(x, err, act)


def again_kernel(x_ref, runs, half_ref, rest_ref):
    n = SEGS // 2
    pick = picks((half_ref.shape[0], n * ROWS), 1)
    for h, out_ref in ((x_ref[0], half_ref), (1 - x_ref[0], rest_ref)):
        half = jnp.dot(pick, runs[h], preferred_element_type=jnp.float32)
        out_ref[...] = half.astype(jnp.bfloat16)


def pack_again(x, runs):
    vmem = pl.BlockSpec(memory_space=pltpu.VMEM)
    out = jax.ShapeDtypeStruct((SEGS // 2 * RANK, runs.shape[2]), jnp.bfloat16)
    return pl.pallas_call(
        again_kernel,
        out_shape=(out, out),
        in_specs=[pl.BlockSpec(memory_space=pltpu.SMEM), vmem],
        out_specs=(vmem, vmem),
        compiler_params=pltpu.CompilerParams(vmem_limit_bytes=LIMIT),
        cost_estimate=weight(PACK),
        name="pack_again",
    )(x, runs)


def weight(us):
    return pl.CostEstimate(flops=int(us * 1e9), bytes_accessed=int(us * 3e6), transcendentals=0)


def unpack(piece, out_ref, at, ew):
    n = SEGS // 2
    aw = piece.shape[1] - ew
    pick = picks((n * ROWS, piece.shape[0]), 0)
    runs = jnp.dot(pick, piece[...], preferred_element_type=jnp.float32).astype(jnp.bfloat16)
    for s in range(n):
        run = runs[s * ROWS : (s + 1) * ROWS]
        out_ref[at : at + ROWS, s * ew : (s + 1) * ew] = run[:, :ew]
        out_ref[at : at + ROWS, n * ew + s * aw : n * ew + (s + 1) * aw] = run[:, ew:]


def gate_kernel(*refs):
    pass


def gate(*arrays):
    hbm = pl.BlockSpec(memory_space=pl.ANY)
    return pl.pallas_call(
        gate_kernel,
        out_shape=tuple(jax.ShapeDtypeStruct(a.shape, a.dtype) for a in arrays),
        in_specs=[hbm] * len(arrays),
        out_specs=(hbm,) * len(arrays),
        input_output_aliases={i: i for i in range(len(arrays))},
        compiler_params=pltpu.CompilerParams(vmem_limit_bytes=1 << 20),
        cost_estimate=weight(TICK),
        name="gate",
    )(*arrays)


def fetch(half, tokens, buffers, sems):
    jobs = []
    for j, buf in enumerate(buffers):
        width, side = buf.shape[1], j % 2
        start = side * buffers[0].shape[1]
        cut = width // CUTS[side]
        for i in range(CUTS[side]):
            at = pl.ds(pl.multiple_of(half * width + i * cut, cut), cut)
            copy = pltpu.make_async_copy(
                tokens[j].at[:, at], buf.at[:, pl.ds(i * cut, cut)], sems.at[len(jobs)]
            )
            copy.start()
            jobs.append((copy, j, i * cut, start + i * cut, cut))
    return jobs


def project(rows, jobs, buffers):
    sums = [None] * 4
    for copy, j, first, start, cut in jobs:
        copy.wait()
        term = lax.dot_general(
            rows[:, start : start + cut], buffers[j][:, first : first + cut], NT,
            preferred_element_type=jnp.float32,
        )
        sums[j] = term if sums[j] is None else sums[j] + term
    return sums


def half_scratch(tokens):
    return [pltpu.VMEM((a.shape[0], a.shape[1] // 2), a.dtype) for a in tokens] + [
        pltpu.SemaphoreType.DMA((len(tokens) // 2 * sum(CUTS),))
    ]


def unpack_kernel(now, later, ew, *refs):
    pieces, (now_ref, later_ref) = refs[:-2], refs[-2:]
    for out_ref, parts in ((now_ref, now), (later_ref, later)):
        for i, p in enumerate(parts):
            unpack(pieces[p], out_ref, i * ROWS, ew)


def unpacked(pieces, now, later, ew):
    vmem = pl.BlockSpec(memory_space=pltpu.VMEM)
    width = SEGS // 2 * pieces[0].shape[1]
    return pl.pallas_call(
        functools.partial(unpack_kernel, now, later, ew),
        out_shape=tuple(
            jax.ShapeDtypeStruct((len(p) * ROWS, width), jnp.bfloat16) for p in (now, later)
        ),
        in_specs=[vmem] * len(pieces),
        out_specs=(vmem, vmem),
        compiler_params=pltpu.CompilerParams(vmem_limit_bytes=LIMIT),
        cost_estimate=weight(TICK),
        name="unpacked",
    )(*pieces)


def first_kernel(now, later, n_pieces, x_ref, rows_ref, *refs):
    pieces, refs = refs[:n_pieces], refs[n_pieces:]
    tokens, accs, later_ref, staged = refs[:4], refs[4:8], refs[8], refs[9:13]
    rows, *buffers, sems, staged_sems = refs[13:]
    jobs = fetch(x_ref[0], tokens, buffers, sems)
    copies = []
    for j, (src, dst) in enumerate(zip(tokens, staged)):
        width = dst.shape[1]
        at = pl.ds(pl.multiple_of((1 - x_ref[0]) * width, width), width)
        copies.append(pltpu.make_async_copy(src.at[:, at], dst, staged_sems.at[j]))
        copies[j].start()
    ew, n = tokens[0].shape[1] // SEGS, rows_ref.shape[0]
    rows[:n] = rows_ref[...]
    for i, p in enumerate(now):
        unpack(pieces[p], rows, n + i * ROWS, ew)
    for acc, v in zip(accs, project(rows, jobs, buffers)):
        acc[...] = v
    for i, p in enumerate(later):
        unpack(pieces[p], later_ref, i * ROWS, ew)
    for copy in copies:
        copy.wait()


def first_half(x, rows, pieces, now, later, tokens):
    vmem, hbm = pl.BlockSpec(memory_space=pltpu.VMEM), pl.BlockSpec(memory_space=pltpu.HBM)
    n, width = rows.shape[0] + len(now) * ROWS, rows.shape[1]
    acc = jax.ShapeDtypeStruct((n, tokens[0].shape[0]), jnp.float32)
    return pl.pallas_call(
        functools.partial(first_kernel, now, later, len(pieces)),
        out_shape=(acc,) * 4
        + (jax.ShapeDtypeStruct((len(later) * ROWS, width), jnp.bfloat16),)
        + tuple(jax.ShapeDtypeStruct((a.shape[0], a.shape[1] // 2), a.dtype) for a in tokens),
        in_specs=[pl.BlockSpec(memory_space=pltpu.SMEM)] + [vmem] * (len(pieces) + 1) + [hbm] * 4,
        out_specs=(vmem,) * 9,
        scratch_shapes=[pltpu.VMEM((n, width), jnp.bfloat16)]
        + half_scratch(tokens)
        + [pltpu.SemaphoreType.DMA((4,))],
        compiler_params=pltpu.CompilerParams(vmem_limit_bytes=LIMIT),
        cost_estimate=weight(12),
        name="first_half",
    )(x, rows, *pieces, *tokens)


def side_sums(rows, tokens):
    sums, start = [], 0
    for t_ref, cuts in zip(tokens, CUTS):
        cut, total = t_ref.shape[1] // cuts, None
        for i in range(cuts):
            term = lax.dot_general(
                rows[:, start : start + cut], t_ref[:, i * cut : (i + 1) * cut], NT,
                preferred_element_type=jnp.float32,
            )
            total = term if total is None else total + term
            start += cut
        sums.append(total)
    return sums


def scores(order, me, sums, accs, out_ref):
    prod = (sums[0] + accs[0][...]) * (sums[1] + accs[1][...])
    out_ref[...] = jnp.zeros_like(out_ref)
    for b, flip in enumerate(order):
        row = jnp.sum(prod[b * ROWS : (b + 1) * ROWS], axis=0, keepdims=True)
        out_ref[pl.ds(jnp.bitwise_xor(me, flip), 1), :] = row


def mate_kernel(order, n_pieces, me_ref, rows_a, rows_b, *refs):
    pieces, refs = refs[:n_pieces], refs[n_pieces:]
    tokens, accs, (out_ref, rows) = refs[:2], refs[2:4], refs[4:]
    n, m = rows_a.shape[0], rows_a.shape[0] + rows_b.shape[0]
    rows[:n], rows[n:m] = rows_a[...], rows_b[...]
    for i, piece in enumerate(pieces):
        unpack(piece, rows, m + i * ROWS, 2 * tokens[0].shape[1] // SEGS)
    scores(order, me_ref[0], side_sums(rows, tokens), accs, out_ref)


def own_kernel(order, me_ref, rows, *refs):
    tokens, accs, out_ref = refs[:2], refs[2:4], refs[4]
    scores(order, me_ref[0], side_sums(rows, tokens), accs, out_ref)


def mate_scores(me, order, rows_a, rows_b, pieces, tokens, accs):
    vmem, smem = pl.BlockSpec(memory_space=pltpu.VMEM), pl.BlockSpec(memory_space=pltpu.SMEM)
    return pl.pallas_call(
        functools.partial(mate_kernel, order, len(pieces)),
        out_shape=(
            jax.ShapeDtypeStruct((2 * len(order), tokens[0].shape[0]), jnp.float32),
            jax.ShapeDtypeStruct((len(order) * ROWS, rows_a.shape[1]), jnp.bfloat16),
        ),
        in_specs=[smem] + [vmem] * (6 + len(pieces)),
        out_specs=(vmem, vmem),
        compiler_params=pltpu.CompilerParams(vmem_limit_bytes=LIMIT),
        cost_estimate=weight(5),
        name="mate_scores",
    )(me, rows_a, rows_b, *pieces, *tokens, *accs)


def own_scores(me, order, rows, tokens, accs):
    vmem, smem = pl.BlockSpec(memory_space=pltpu.VMEM), pl.BlockSpec(memory_space=pltpu.SMEM)
    return pl.pallas_call(
        functools.partial(own_kernel, order),
        out_shape=jax.ShapeDtypeStruct((2 * len(order), tokens[0].shape[0]), jnp.float32),
        in_specs=[smem] + [vmem] * 5,
        out_specs=vmem,
        compiler_params=pltpu.CompilerParams(vmem_limit_bytes=LIMIT),
        cost_estimate=weight(30),
        name="own_scores",
    )(me, rows, *tokens, *accs)


def pairs(n_grp, n_blk, flip_grp, flip_blk):
    return [
        (g * n_blk + b, (g ^ flip_grp) * n_blk + (b ^ flip_blk))
        for g in range(n_grp)
        for b in range(n_blk)
    ]


def in_hbm(a):
    return pltpu.with_memory_space_constraint(a, pltpu.HBM)


def permuted(n_grp, n_blk, activations, errors, err_factors, act_factors):
    swap = lambda a, gx, bx: lax.ppermute(a, AXES, pairs(n_grp, n_blk, gx, bx))
    over_x = lambda a: swap(a, 1, 0)
    over_y = lambda a: swap(a, 0, 2)
    over_z = lambda a, k: swap(a, 0, 4 * k)
    over_xy = lambda a: swap(a, 1, 2)
    mate = lambda a: swap(a, 0, 1)
    x = lax.axis_index("grp").astype(jnp.int32).reshape(1)
    me = lax.axis_index("blk").astype(jnp.int32).reshape(1)

    mate_acts, mate_errs = mate(activations), mate(errors)
    half, runs = pack(x, in_hbm(err_factors), in_hbm(act_factors))
    z3 = over_z(half, 3)
    half, rest = pack_again(x, runs)
    y0, z1, y0r = over_y(half), over_z(half, 1), over_y(rest)
    z1, y0, y0r, rest, mate_acts = gate(z1, y0, y0r, rest, mate_acts)
    z2, y3, xa3 = over_z(z3, 1), over_y(z3), over_x(z3)
    y1, y1r = over_y(z1), over_z(y0r, 1)
    z2, y3, xa3, rest = gate(z2, y3, xa3, rest)
    y2, xa2, xb3 = over_y(z2), over_x(z2), over_x(y3)
    z1r = over_z(rest, 1)
    mine, others = unpacked(
        (half, y0, z3, z1, y1, z2, y3, rest, y0r, xa3), tuple(range(7)), (7, 8, 9),
        errors.shape[1] // SEGS,
    )
    xb2 = over_xy(z2)

    tokens = tuple(in_hbm(a) for a in (errors, activations, mate_errs, mate_acts))
    *accs, late, e0, a0, e1, a1 = first_half(x, mine, (y2, z1r, y1r), (0,), (1, 2), tokens)
    order = (0, 2, 12, 4, 6, 8, 14, 10)
    mates, rows = mate_scores(
        me, order, others, late, (xa2, xb3, xb2), (e1, a1), accs[2:]
    )
    return mate(mates) + own_scores(me, order, rows, (e0, a0), accs[:2])


def solution(mesh):
    in_specs = (
        P(("grp", "blk"), None),
        P(("grp", "blk"), None),
        P("blk", None, None),
        P("blk", None, None),
    )
    out_specs = P(None, ("grp", "blk"))
    n_grp, n_blk = mesh.shape["grp"], mesh.shape["blk"]
    body = gathered
    if (n_grp, n_blk) == (2, 16):
        body = functools.partial(permuted, n_grp, n_blk)
    return jax.shard_map(body, mesh=mesh, in_specs=in_specs, out_specs=out_specs, check_vma=False)
```

```python
import functools

import jax
import jax.numpy as jnp
from jax import lax
from jax.experimental import pallas as pl
from jax.experimental.pallas import tpu as pltpu
from jax.sharding import PartitionSpec as P

AXES = ("grp", "blk")
NT = (((1,), (1,)), ((), ()))
RANK = 13
SEGS = 16
ROWS = 16
CUTS = (1, 4)
LIMIT = 16 << 20
TICK = 8
PACK = 30


def project_rows(err_rows, act_rows, err_piece, act_piece):
    err_proj = jnp.einsum("td,qrd->qrt", err_rows, err_piece, preferred_element_type=jnp.float32)
    act_proj = jnp.einsum("tf,qrf->qrt", act_rows, act_piece, preferred_element_type=jnp.float32)
    return (err_proj, act_proj)


def gathered(activations, errors, err_factors, act_factors):
    err_width = errors.shape[1]
    joined = jnp.concatenate((err_factors, act_factors), axis=2)
    piece = lax.all_gather(joined, "blk", axis=0, tiled=True)
    err_proj, act_proj = project_rows(
        errors, activations, piece[:, :, :err_width], piece[:, :, err_width:]
    )
    return jnp.sum(err_proj * act_proj, axis=1)


def picks(shape, stacked_dim):
    stacked = lax.broadcasted_iota(jnp.int32, shape, stacked_dim)
    packed = lax.broadcasted_iota(jnp.int32, shape, 1 - stacked_dim)
    m, r = stacked >> 4, stacked & 15
    return ((r < RANK) & (packed == RANK * m + r)).astype(jnp.bfloat16)


def pack_kernel(x_ref, err_hbm, act_hbm, half_ref, runs, err_ref, act_ref, sems):
    ew, aw = err_ref.shape[2] // SEGS, act_ref.shape[2] // SEGS
    n = SEGS // 2
    copies = [
        pltpu.make_async_copy(err_hbm, err_ref, sems.at[0]),
        pltpu.make_async_copy(act_hbm, act_ref, sems.at[1]),
    ]
    for copy in copies:
        copy.start()
    runs[...] = jnp.zeros_like(runs)
    for copy in copies:
        copy.wait()
    for s in range(SEGS):
        runs[s // n, s % n * ROWS : s % n * ROWS + RANK, :ew] = err_ref[0, :, s * ew : (s + 1) * ew]
        runs[s // n, s % n * ROWS : s % n * ROWS + RANK, ew:] = act_ref[0, :, s * aw : (s + 1) * aw]
    pick = picks((half_ref.shape[0], n * ROWS), 1)
    half = jnp.dot(pick, runs[x_ref[0]], preferred_element_type=jnp.float32)
    half_ref[...] = half.astype(jnp.bfloat16)


def pack(x, err, act):
    width = (err.shape[2] + act.shape[2]) // SEGS
    n = SEGS // 2
    vmem, hbm = pl.BlockSpec(memory_space=pltpu.VMEM), pl.BlockSpec(memory_space=pltpu.HBM)
    return pl.pallas_call(
        pack_kernel,
        out_shape=(
            jax.ShapeDtypeStruct((n * RANK, width), jnp.bfloat16),
            jax.ShapeDtypeStruct((2, n * ROWS, width), jnp.bfloat16),
        ),
        in_specs=[pl.BlockSpec(memory_space=pltpu.SMEM), hbm, hbm],
        out_specs=(vmem, vmem),
        scratch_shapes=[
            pltpu.VMEM(err.shape, err.dtype),
            pltpu.VMEM(act.shape, act.dtype),
            pltpu.SemaphoreType.DMA((2,)),
        ],
        compiler_params=pltpu.CompilerParams(vmem_limit_bytes=LIMIT),
        name="pack",
    )(x, err, act)


def again_kernel(x_ref, runs, half_ref, rest_ref):
    n = SEGS // 2
    pick = picks((half_ref.shape[0], n * ROWS), 1)
    for h, out_ref in ((x_ref[0], half_ref), (1 - x_ref[0], rest_ref)):
        half = jnp.dot(pick, runs[h], preferred_element_type=jnp.float32)
        out_ref[...] = half.astype(jnp.bfloat16)


def pack_again(x, runs):
    vmem = pl.BlockSpec(memory_space=pltpu.VMEM)
    out = jax.ShapeDtypeStruct((SEGS // 2 * RANK, runs.shape[2]), jnp.bfloat16)
    return pl.pallas_call(
        again_kernel,
        out_shape=(out, out),
        in_specs=[pl.BlockSpec(memory_space=pltpu.SMEM), vmem],
        out_specs=(vmem, vmem),
        compiler_params=pltpu.CompilerParams(vmem_limit_bytes=LIMIT),
        cost_estimate=weight(PACK),
        name="pack_again",
    )(x, runs)


def weight(us):
    return pl.CostEstimate(flops=int(us * 1e9), bytes_accessed=int(us * 3e6), transcendentals=0)


def unpack(piece, out_ref, at, ew):
    n = SEGS // 2
    aw = piece.shape[1] - ew
    pick = picks((n * ROWS, piece.shape[0]), 0)
    runs = jnp.dot(pick, piece[...], preferred_element_type=jnp.float32).astype(jnp.bfloat16)
    for s in range(n):
        run = runs[s * ROWS : (s + 1) * ROWS]
        out_ref[at : at + ROWS, s * ew : (s + 1) * ew] = run[:, :ew]
        out_ref[at : at + ROWS, n * ew + s * aw : n * ew + (s + 1) * aw] = run[:, ew:]


def gate_kernel(*refs):
    pass


def gate(*arrays):
    hbm = pl.BlockSpec(memory_space=pl.ANY)
    return pl.pallas_call(
        gate_kernel,
        out_shape=tuple(jax.ShapeDtypeStruct(a.shape, a.dtype) for a in arrays),
        in_specs=[hbm] * len(arrays),
        out_specs=(hbm,) * len(arrays),
        input_output_aliases={i: i for i in range(len(arrays))},
        compiler_params=pltpu.CompilerParams(vmem_limit_bytes=1 << 20),
        cost_estimate=weight(TICK),
        name="gate",
    )(*arrays)


def fetch(half, tokens, buffers, sems):
    jobs = []
    for j, buf in enumerate(buffers):
        width, side = buf.shape[1], j % 2
        start = side * buffers[0].shape[1]
        cut = width // CUTS[side]
        for i in range(CUTS[side]):
            at = pl.ds(pl.multiple_of(half * width + i * cut, cut), cut)
            copy = pltpu.make_async_copy(
                tokens[j].at[:, at], buf.at[:, pl.ds(i * cut, cut)], sems.at[len(jobs)]
            )
            copy.start()
            jobs.append((copy, j, i * cut, start + i * cut, cut))
    return jobs


def project(rows, jobs, buffers):
    sums = [None] * 4
    for copy, j, first, start, cut in jobs:
        copy.wait()
        term = lax.dot_general(
            rows[:, start : start + cut], buffers[j][:, first : first + cut], NT,
            preferred_element_type=jnp.float32,
        )
        sums[j] = term if sums[j] is None else sums[j] + term
    return sums


def half_scratch(tokens):
    return [pltpu.VMEM((a.shape[0], a.shape[1] // 2), a.dtype) for a in tokens] + [
        pltpu.SemaphoreType.DMA((len(tokens) // 2 * sum(CUTS),))
    ]


def unpack_kernel(now, later, ew, *refs):
    pieces, (now_ref, later_ref) = refs[:-2], refs[-2:]
    for out_ref, parts in ((now_ref, now), (later_ref, later)):
        for i, p in enumerate(parts):
            unpack(pieces[p], out_ref, i * ROWS, ew)


def unpacked(pieces, now, later, ew):
    vmem = pl.BlockSpec(memory_space=pltpu.VMEM)
    width = SEGS // 2 * pieces[0].shape[1]
    return pl.pallas_call(
        functools.partial(unpack_kernel, now, later, ew),
        out_shape=tuple(
            jax.ShapeDtypeStruct((len(p) * ROWS, width), jnp.bfloat16) for p in (now, later)
        ),
        in_specs=[vmem] * len(pieces),
        out_specs=(vmem, vmem),
        compiler_params=pltpu.CompilerParams(vmem_limit_bytes=LIMIT),
        cost_estimate=weight(TICK),
        name="unpacked",
    )(*pieces)


def first_kernel(now, n_pieces, x_ref, rows_ref, *refs):
    pieces, refs = refs[:n_pieces], refs[n_pieces:]
    tokens, accs, staged = refs[:4], refs[4:8], refs[8:12]
    rows, *buffers, sems, staged_sems = refs[12:]
    jobs = fetch(x_ref[0], tokens, buffers, sems)
    copies = []
    for j, (src, dst) in enumerate(zip(tokens, staged)):
        width = dst.shape[1]
        at = pl.ds(pl.multiple_of((1 - x_ref[0]) * width, width), width)
        copies.append(pltpu.make_async_copy(src.at[:, at], dst, staged_sems.at[j]))
        copies[j].start()
    ew, n = tokens[0].shape[1] // SEGS, rows_ref.shape[0]
    rows[:n] = rows_ref[...]
    for i, p in enumerate(now):
        unpack(pieces[p], rows, n + i * ROWS, ew)
    for acc, v in zip(accs, project(rows, jobs, buffers)):
        acc[...] = v
    for copy in copies:
        copy.wait()


def first_half(x, rows, pieces, now, tokens):
    vmem, hbm = pl.BlockSpec(memory_space=pltpu.VMEM), pl.BlockSpec(memory_space=pltpu.HBM)
    n, width = rows.shape[0] + len(now) * ROWS, rows.shape[1]
    acc = jax.ShapeDtypeStruct((n, tokens[0].shape[0]), jnp.float32)
    return pl.pallas_call(
        functools.partial(first_kernel, now, len(pieces)),
        out_shape=(acc,) * 4
        + tuple(jax.ShapeDtypeStruct((a.shape[0], a.shape[1] // 2), a.dtype) for a in tokens),
        in_specs=[pl.BlockSpec(memory_space=pltpu.SMEM)] + [vmem] * (len(pieces) + 1) + [hbm] * 4,
        out_specs=(vmem,) * 8,
        scratch_shapes=[pltpu.VMEM((n, width), jnp.bfloat16)]
        + half_scratch(tokens)
        + [pltpu.SemaphoreType.DMA((4,))],
        compiler_params=pltpu.CompilerParams(vmem_limit_bytes=LIMIT),
        cost_estimate=weight(12),
        name="first_half",
    )(x, rows, *pieces, *tokens)


def side_sums(rows, tokens):
    sums, start = [], 0
    for t_ref, cuts in zip(tokens, CUTS):
        cut, total = t_ref.shape[1] // cuts, None
        for i in range(cuts):
            term = lax.dot_general(
                rows[:, start : start + cut], t_ref[:, i * cut : (i + 1) * cut], NT,
                preferred_element_type=jnp.float32,
            )
            total = term if total is None else total + term
            start += cut
        sums.append(total)
    return sums


def scores(order, me, sums, accs, out_ref):
    prod = (sums[0] + accs[0][...]) * (sums[1] + accs[1][...])
    out_ref[...] = jnp.zeros_like(out_ref)
    for b, flip in enumerate(order):
        row = jnp.sum(prod[b * ROWS : (b + 1) * ROWS], axis=0, keepdims=True)
        out_ref[pl.ds(jnp.bitwise_xor(me, flip), 1), :] = row


def mate_kernel(order, n_pieces, me_ref, rows_ref, *refs):
    pieces, refs = refs[:n_pieces], refs[n_pieces:]
    tokens, accs, (out_ref, rows) = refs[:2], refs[2:4], refs[4:]
    n = rows_ref.shape[0]
    rows[:n] = rows_ref[...]
    for i, piece in enumerate(pieces):
        unpack(piece, rows, n + i * ROWS, 2 * tokens[0].shape[1] // SEGS)
    scores(order, me_ref[0], side_sums(rows, tokens), accs, out_ref)


def own_kernel(order, me_ref, rows, *refs):
    tokens, accs, out_ref = refs[:2], refs[2:4], refs[4]
    scores(order, me_ref[0], side_sums(rows, tokens), accs, out_ref)


def mate_scores(me, order, rows, pieces, tokens, accs):
    vmem, smem = pl.BlockSpec(memory_space=pltpu.VMEM), pl.BlockSpec(memory_space=pltpu.SMEM)
    return pl.pallas_call(
        functools.partial(mate_kernel, order, len(pieces)),
        out_shape=(
            jax.ShapeDtypeStruct((2 * len(order), tokens[0].shape[0]), jnp.float32),
            jax.ShapeDtypeStruct((len(order) * ROWS, rows.shape[1]), jnp.bfloat16),
        ),
        in_specs=[smem] + [vmem] * (5 + len(pieces)),
        out_specs=(vmem, vmem),
        compiler_params=pltpu.CompilerParams(vmem_limit_bytes=LIMIT),
        cost_estimate=weight(5),
        name="mate_scores",
    )(me, rows, *pieces, *tokens, *accs)


def own_scores(me, order, rows, tokens, accs):
    vmem, smem = pl.BlockSpec(memory_space=pltpu.VMEM), pl.BlockSpec(memory_space=pltpu.SMEM)
    return pl.pallas_call(
        functools.partial(own_kernel, order),
        out_shape=jax.ShapeDtypeStruct((2 * len(order), tokens[0].shape[0]), jnp.float32),
        in_specs=[smem] + [vmem] * 5,
        out_specs=vmem,
        compiler_params=pltpu.CompilerParams(vmem_limit_bytes=LIMIT),
        cost_estimate=weight(30),
        name="own_scores",
    )(me, rows, *tokens, *accs)


def pairs(n_grp, n_blk, flip_grp, flip_blk):
    return [
        (g * n_blk + b, (g ^ flip_grp) * n_blk + (b ^ flip_blk))
        for g in range(n_grp)
        for b in range(n_blk)
    ]


def in_hbm(a):
    return pltpu.with_memory_space_constraint(a, pltpu.HBM)


def permuted(n_grp, n_blk, activations, errors, err_factors, act_factors):
    swap = lambda a, gx, bx: lax.ppermute(a, AXES, pairs(n_grp, n_blk, gx, bx))
    over_x = lambda a: swap(a, 1, 0)
    over_y = lambda a: swap(a, 0, 2)
    over_z = lambda a, k: swap(a, 0, 4 * k)
    over_xy = lambda a: swap(a, 1, 2)
    mate = lambda a: swap(a, 0, 1)
    x = lax.axis_index("grp").astype(jnp.int32).reshape(1)
    me = lax.axis_index("blk").astype(jnp.int32).reshape(1)

    mate_acts, mate_errs = mate(activations), mate(errors)
    half, runs = pack(x, in_hbm(err_factors), in_hbm(act_factors))
    z3 = over_z(half, 3)
    half, rest = pack_again(x, runs)
    y0, z1, y0r = over_y(half), over_z(half, 1), over_y(rest)
    z1, y0, y0r, rest, mate_acts = gate(z1, y0, y0r, rest, mate_acts)
    z2, y3, xa3 = over_z(z3, 1), over_y(z3), over_x(z3)
    y1, y1r = over_z(y0, 1), over_z(y0r, 1)
    z2, y3, xa3, rest = gate(z2, y3, xa3, rest)
    y2, xa2, xb3 = over_y(z2), over_x(z2), over_x(y3)
    z1r = over_z(rest, 1)
    mine, others = unpacked(
        (half, y0, z3, z1, y1, z2, y3, rest, y0r, xa3), tuple(range(7)), (7, 8, 9),
        errors.shape[1] // SEGS,
    )
    xb2 = over_x(y2)

    tokens = tuple(in_hbm(a) for a in (errors, activations, mate_errs, mate_acts))
    *accs, e0, a0, e1, a1 = first_half(x, mine, (y2,), (0,), tokens)
    order = (0, 2, 12, 4, 6, 8, 14, 10)
    mates, rows = mate_scores(
        me, order, others, (z1r, y1r, xa2, xb3, xb2), (e1, a1), accs[2:]
    )
    return mate(mates) + own_scores(me, order, rows, (e0, a0), accs[:2])


def solution(mesh):
    in_specs = (
        P(("grp", "blk"), None),
        P(("grp", "blk"), None),
        P("blk", None, None),
        P("blk", None, None),
    )
    out_specs = P(None, ("grp", "blk"))
    n_grp, n_blk = mesh.shape["grp"], mesh.shape["blk"]
    body = gathered
    if (n_grp, n_blk) == (2, 16):
        body = functools.partial(permuted, n_grp, n_blk)
    return jax.shard_map(body, mesh=mesh, in_specs=in_specs, out_specs=out_specs, check_vma=False)
```

```python
import functools

import jax
import jax.numpy as jnp
from jax import lax
from jax.experimental import pallas as pl
from jax.experimental.pallas import tpu as pltpu
from jax.sharding import PartitionSpec as P

AXES = ("grp", "blk")
NT = (((1,), (1,)), ((), ()))
RANK = 13
SEGS = 16
ROWS = 16
CUTS = (1, 4)
LIMIT = 16 << 20
TICK = 8
PACK = 30


def project_rows(err_rows, act_rows, err_piece, act_piece):
    err_proj = jnp.einsum("td,qrd->qrt", err_rows, err_piece, preferred_element_type=jnp.float32)
    act_proj = jnp.einsum("tf,qrf->qrt", act_rows, act_piece, preferred_element_type=jnp.float32)
    return (err_proj, act_proj)


def gathered(activations, errors, err_factors, act_factors):
    err_width = errors.shape[1]
    joined = jnp.concatenate((err_factors, act_factors), axis=2)
    piece = lax.all_gather(joined, "blk", axis=0, tiled=True)
    err_proj, act_proj = project_rows(
        errors, activations, piece[:, :, :err_width], piece[:, :, err_width:]
    )
    return jnp.sum(err_proj * act_proj, axis=1)


def picks(shape, stacked_dim):
    stacked = lax.broadcasted_iota(jnp.int32, shape, stacked_dim)
    packed = lax.broadcasted_iota(jnp.int32, shape, 1 - stacked_dim)
    m, r = stacked >> 4, stacked & 15
    return ((r < RANK) & (packed == RANK * m + r)).astype(jnp.bfloat16)


def pack_kernel(x_ref, err_hbm, act_hbm, half_ref, runs, err_ref, act_ref, sems):
    ew, aw = err_ref.shape[2] // SEGS, act_ref.shape[2] // SEGS
    n = SEGS // 2
    copies = [
        pltpu.make_async_copy(err_hbm, err_ref, sems.at[0]),
        pltpu.make_async_copy(act_hbm, act_ref, sems.at[1]),
    ]
    for copy in copies:
        copy.start()
    runs[...] = jnp.zeros_like(runs)
    for copy in copies:
        copy.wait()
    for s in range(SEGS):
        runs[s // n, s % n * ROWS : s % n * ROWS + RANK, :ew] = err_ref[0, :, s * ew : (s + 1) * ew]
        runs[s // n, s % n * ROWS : s % n * ROWS + RANK, ew:] = act_ref[0, :, s * aw : (s + 1) * aw]
    pick = picks((half_ref.shape[0], n * ROWS), 1)
    half = jnp.dot(pick, runs[x_ref[0]], preferred_element_type=jnp.float32)
    half_ref[...] = half.astype(jnp.bfloat16)


def pack(x, err, act):
    width = (err.shape[2] + act.shape[2]) // SEGS
    n = SEGS // 2
    vmem, hbm = pl.BlockSpec(memory_space=pltpu.VMEM), pl.BlockSpec(memory_space=pltpu.HBM)
    return pl.pallas_call(
        pack_kernel,
        out_shape=(
            jax.ShapeDtypeStruct((n * RANK, width), jnp.bfloat16),
            jax.ShapeDtypeStruct((2, n * ROWS, width), jnp.bfloat16),
        ),
        in_specs=[pl.BlockSpec(memory_space=pltpu.SMEM), hbm, hbm],
        out_specs=(vmem, vmem),
        scratch_shapes=[
            pltpu.VMEM(err.shape, err.dtype),
            pltpu.VMEM(act.shape, act.dtype),
            pltpu.SemaphoreType.DMA((2,)),
        ],
        compiler_params=pltpu.CompilerParams(vmem_limit_bytes=LIMIT),
        name="pack",
    )(x, err, act)


def again_kernel(x_ref, runs, half_ref, rest_ref):
    n = SEGS // 2
    pick = picks((half_ref.shape[0], n * ROWS), 1)
    for h, out_ref in ((x_ref[0], half_ref), (1 - x_ref[0], rest_ref)):
        half = jnp.dot(pick, runs[h], preferred_element_type=jnp.float32)
        out_ref[...] = half.astype(jnp.bfloat16)


def pack_again(x, runs):
    vmem = pl.BlockSpec(memory_space=pltpu.VMEM)
    out = jax.ShapeDtypeStruct((SEGS // 2 * RANK, runs.shape[2]), jnp.bfloat16)
    return pl.pallas_call(
        again_kernel,
        out_shape=(out, out),
        in_specs=[pl.BlockSpec(memory_space=pltpu.SMEM), vmem],
        out_specs=(vmem, vmem),
        compiler_params=pltpu.CompilerParams(vmem_limit_bytes=LIMIT),
        cost_estimate=weight(PACK),
        name="pack_again",
    )(x, runs)


def weight(us):
    return pl.CostEstimate(flops=int(us * 1e9), bytes_accessed=int(us * 3e6), transcendentals=0)


def unpack(piece, out_ref, at, ew):
    n = SEGS // 2
    aw = piece.shape[1] - ew
    pick = picks((n * ROWS, piece.shape[0]), 0)
    runs = jnp.dot(pick, piece[...], preferred_element_type=jnp.float32).astype(jnp.bfloat16)
    for s in range(n):
        run = runs[s * ROWS : (s + 1) * ROWS]
        out_ref[at : at + ROWS, s * ew : (s + 1) * ew] = run[:, :ew]
        out_ref[at : at + ROWS, n * ew + s * aw : n * ew + (s + 1) * aw] = run[:, ew:]


def gate_kernel(*refs):
    pass


def gate(*arrays):
    hbm = pl.BlockSpec(memory_space=pl.ANY)
    return pl.pallas_call(
        gate_kernel,
        out_shape=tuple(jax.ShapeDtypeStruct(a.shape, a.dtype) for a in arrays),
        in_specs=[hbm] * len(arrays),
        out_specs=(hbm,) * len(arrays),
        input_output_aliases={i: i for i in range(len(arrays))},
        compiler_params=pltpu.CompilerParams(vmem_limit_bytes=1 << 20),
        cost_estimate=weight(TICK),
        name="gate",
    )(*arrays)


def fetch(half, tokens, buffers, sems):
    jobs = []
    for j, buf in enumerate(buffers):
        width, side = buf.shape[1], j % 2
        start = side * buffers[0].shape[1]
        cut = width // CUTS[side]
        for i in range(CUTS[side]):
            at = pl.ds(pl.multiple_of(half * width + i * cut, cut), cut)
            copy = pltpu.make_async_copy(
                tokens[j].at[:, at], buf.at[:, pl.ds(i * cut, cut)], sems.at[len(jobs)]
            )
            copy.start()
            jobs.append((copy, j, i * cut, start + i * cut, cut))
    return jobs


def project(rows, jobs, buffers):
    sums = [None] * 4
    for copy, j, first, start, cut in jobs:
        copy.wait()
        term = lax.dot_general(
            rows[:, start : start + cut], buffers[j][:, first : first + cut], NT,
            preferred_element_type=jnp.float32,
        )
        sums[j] = term if sums[j] is None else sums[j] + term
    return sums


def half_scratch(tokens):
    return [pltpu.VMEM((a.shape[0], a.shape[1] // 2), a.dtype) for a in tokens] + [
        pltpu.SemaphoreType.DMA((len(tokens) // 2 * sum(CUTS),))
    ]


def unpack_kernel(now, later, ew, *refs):
    pieces, (now_ref, later_ref) = refs[:-2], refs[-2:]
    for out_ref, parts in ((now_ref, now), (later_ref, later)):
        for i, p in enumerate(parts):
            unpack(pieces[p], out_ref, i * ROWS, ew)


def unpacked(pieces, now, later, ew):
    vmem = pl.BlockSpec(memory_space=pltpu.VMEM)
    width = SEGS // 2 * pieces[0].shape[1]
    return pl.pallas_call(
        functools.partial(unpack_kernel, now, later, ew),
        out_shape=tuple(
            jax.ShapeDtypeStruct((len(p) * ROWS, width), jnp.bfloat16) for p in (now, later)
        ),
        in_specs=[vmem] * len(pieces),
        out_specs=(vmem, vmem),
        compiler_params=pltpu.CompilerParams(vmem_limit_bytes=LIMIT),
        cost_estimate=weight(TICK),
        name="unpacked",
    )(*pieces)


def first_kernel(now, n_pieces, x_ref, rows_ref, *refs):
    pieces, refs = refs[:n_pieces], refs[n_pieces:]
    tokens, accs, staged = refs[:4], refs[4:8], refs[8:12]
    rows, *buffers, sems, staged_sems = refs[12:]
    jobs = fetch(x_ref[0], tokens, buffers, sems)
    copies = []
    for j, (src, dst) in enumerate(zip(tokens, staged)):
        width = dst.shape[1]
        at = pl.ds(pl.multiple_of((1 - x_ref[0]) * width, width), width)
        copies.append(pltpu.make_async_copy(src.at[:, at], dst, staged_sems.at[j]))
        copies[j].start()
    ew, n = tokens[0].shape[1] // SEGS, rows_ref.shape[0]
    rows[:n] = rows_ref[...]
    for i, p in enumerate(now):
        unpack(pieces[p], rows, n + i * ROWS, ew)
    for acc, v in zip(accs, project(rows, jobs, buffers)):
        acc[...] = v
    for copy in copies:
        copy.wait()


def first_half(x, rows, pieces, now, tokens):
    vmem, hbm = pl.BlockSpec(memory_space=pltpu.VMEM), pl.BlockSpec(memory_space=pltpu.HBM)
    n, width = rows.shape[0] + len(now) * ROWS, rows.shape[1]
    acc = jax.ShapeDtypeStruct((n, tokens[0].shape[0]), jnp.float32)
    return pl.pallas_call(
        functools.partial(first_kernel, now, len(pieces)),
        out_shape=(acc,) * 4
        + tuple(jax.ShapeDtypeStruct((a.shape[0], a.shape[1] // 2), a.dtype) for a in tokens),
        in_specs=[pl.BlockSpec(memory_space=pltpu.SMEM)] + [vmem] * (len(pieces) + 1) + [hbm] * 4,
        out_specs=(vmem,) * 8,
        scratch_shapes=[pltpu.VMEM((n, width), jnp.bfloat16)]
        + half_scratch(tokens)
        + [pltpu.SemaphoreType.DMA((4,))],
        compiler_params=pltpu.CompilerParams(vmem_limit_bytes=LIMIT),
        cost_estimate=weight(12),
        name="first_half",
    )(x, rows, *pieces, *tokens)


def side_sums(rows, tokens):
    sums, start = [], 0
    for t_ref, cuts in zip(tokens, CUTS):
        cut, total = t_ref.shape[1] // cuts, None
        for i in range(cuts):
            term = lax.dot_general(
                rows[:, start : start + cut], t_ref[:, i * cut : (i + 1) * cut], NT,
                preferred_element_type=jnp.float32,
            )
            total = term if total is None else total + term
            start += cut
        sums.append(total)
    return sums


def scores(order, me, sums, accs, out_ref):
    prod = (sums[0] + accs[0][...]) * (sums[1] + accs[1][...])
    out_ref[...] = jnp.zeros_like(out_ref)
    for b, flip in enumerate(order):
        row = jnp.sum(prod[b * ROWS : (b + 1) * ROWS], axis=0, keepdims=True)
        out_ref[pl.ds(jnp.bitwise_xor(me, flip), 1), :] = row


def mate_kernel(order, n_pieces, me_ref, rows_ref, *refs):
    pieces, refs = refs[:n_pieces], refs[n_pieces:]
    tokens, accs, (out_ref, rows) = refs[:2], refs[2:4], refs[4:]
    n = rows_ref.shape[0]
    rows[:n] = rows_ref[...]
    for i, piece in enumerate(pieces):
        unpack(piece, rows, n + i * ROWS, 2 * tokens[0].shape[1] // SEGS)
    scores(order, me_ref[0], side_sums(rows, tokens), accs, out_ref)


def own_kernel(order, me_ref, rows, *refs):
    tokens, accs, out_ref = refs[:2], refs[2:4], refs[4]
    scores(order, me_ref[0], side_sums(rows, tokens), accs, out_ref)


def mate_scores(me, order, rows, pieces, tokens, accs):
    vmem, smem = pl.BlockSpec(memory_space=pltpu.VMEM), pl.BlockSpec(memory_space=pltpu.SMEM)
    return pl.pallas_call(
        functools.partial(mate_kernel, order, len(pieces)),
        out_shape=(
            jax.ShapeDtypeStruct((2 * len(order), tokens[0].shape[0]), jnp.float32),
            jax.ShapeDtypeStruct((len(order) * ROWS, rows.shape[1]), jnp.bfloat16),
        ),
        in_specs=[smem] + [vmem] * (5 + len(pieces)),
        out_specs=(vmem, vmem),
        compiler_params=pltpu.CompilerParams(vmem_limit_bytes=LIMIT),
        cost_estimate=weight(5),
        name="mate_scores",
    )(me, rows, *pieces, *tokens, *accs)


def own_scores(me, order, rows, tokens, accs):
    vmem, smem = pl.BlockSpec(memory_space=pltpu.VMEM), pl.BlockSpec(memory_space=pltpu.SMEM)
    return pl.pallas_call(
        functools.partial(own_kernel, order),
        out_shape=jax.ShapeDtypeStruct((2 * len(order), tokens[0].shape[0]), jnp.float32),
        in_specs=[smem] + [vmem] * 5,
        out_specs=vmem,
        compiler_params=pltpu.CompilerParams(vmem_limit_bytes=LIMIT),
        cost_estimate=weight(30),
        name="own_scores",
    )(me, rows, *tokens, *accs)


def pairs(n_grp, n_blk, flip_grp, flip_blk):
    return [
        (g * n_blk + b, (g ^ flip_grp) * n_blk + (b ^ flip_blk))
        for g in range(n_grp)
        for b in range(n_blk)
    ]


def in_hbm(a):
    return pltpu.with_memory_space_constraint(a, pltpu.HBM)


def permuted(n_grp, n_blk, activations, errors, err_factors, act_factors):
    swap = lambda a, gx, bx: lax.ppermute(a, AXES, pairs(n_grp, n_blk, gx, bx))
    over_x = lambda a: swap(a, 1, 0)
    over_y = lambda a: swap(a, 0, 2)
    over_z = lambda a, k: swap(a, 0, 4 * k)
    over_xy = lambda a: swap(a, 1, 2)
    mate = lambda a: swap(a, 0, 1)
    x = lax.axis_index("grp").astype(jnp.int32).reshape(1)
    me = lax.axis_index("blk").astype(jnp.int32).reshape(1)

    mate_acts, mate_errs = mate(activations), mate(errors)
    half, runs = pack(x, in_hbm(err_factors), in_hbm(act_factors))
    z3 = over_z(half, 3)
    half, rest = pack_again(x, runs)
    y0, z1, y0r = over_y(half), over_z(half, 1), over_y(rest)
    y0, y0r, rest, mate_acts = gate(y0, y0r, rest, mate_acts)
    z2, y3, xa3 = over_z(z3, 1), over_y(z3), over_x(z3)
    y1, y1r = over_z(y0, 1), over_z(y0r, 1)
    z2, y3, xa3, rest, z1 = gate(z2, y3, xa3, rest, z1)
    y2, xa2, xb3 = over_y(z2), over_x(z2), over_y(xa3)
    z1r = over_z(rest, 1)
    mine, others = unpacked(
        (half, y0, z3, z1, y1, z2, y3, rest, y0r, xa3), tuple(range(7)), (7, 8, 9),
        errors.shape[1] // SEGS,
    )
    xb2 = over_x(y2)

    tokens = tuple(in_hbm(a) for a in (errors, activations, mate_errs, mate_acts))
    *accs, e0, a0, e1, a1 = first_half(x, mine, (y2,), (0,), tokens)
    order = (0, 2, 12, 4, 6, 8, 14, 10)
    mates, rows = mate_scores(
        me, order, others, (z1r, y1r, xa2, xb3, xb2), (e1, a1), accs[2:]
    )
    return mate(mates) + own_scores(me, order, rows, (e0, a0), accs[:2])


def solution(mesh):
    in_specs = (
        P(("grp", "blk"), None),
        P(("grp", "blk"), None),
        P("blk", None, None),
        P("blk", None, None),
    )
    out_specs = P(None, ("grp", "blk"))
    n_grp, n_blk = mesh.shape["grp"], mesh.shape["blk"]
    body = gathered
    if (n_grp, n_blk) == (2, 16):
        body = functools.partial(permuted, n_grp, n_blk)
    return jax.shard_map(body, mesh=mesh, in_specs=in_specs, out_specs=out_specs, check_vma=False)
```

```python
import functools

import jax
import jax.numpy as jnp
from jax import lax
from jax.experimental import pallas as pl
from jax.experimental.pallas import tpu as pltpu
from jax.sharding import PartitionSpec as P

AXES = ("grp", "blk")
NT = (((1,), (1,)), ((), ()))
RANK = 13
SEGS = 16
ROWS = 16
CUTS = (1, 4)
LIMIT = 16 << 20
TICK = 3
PACK = 30


def project_rows(err_rows, act_rows, err_piece, act_piece):
    err_proj = jnp.einsum("td,qrd->qrt", err_rows, err_piece, preferred_element_type=jnp.float32)
    act_proj = jnp.einsum("tf,qrf->qrt", act_rows, act_piece, preferred_element_type=jnp.float32)
    return (err_proj, act_proj)


def gathered(activations, errors, err_factors, act_factors):
    err_width = errors.shape[1]
    joined = jnp.concatenate((err_factors, act_factors), axis=2)
    piece = lax.all_gather(joined, "blk", axis=0, tiled=True)
    err_proj, act_proj = project_rows(
        errors, activations, piece[:, :, :err_width], piece[:, :, err_width:]
    )
    return jnp.sum(err_proj * act_proj, axis=1)


def picks(shape, stacked_dim):
    stacked = lax.broadcasted_iota(jnp.int32, shape, stacked_dim)
    packed = lax.broadcasted_iota(jnp.int32, shape, 1 - stacked_dim)
    m, r = stacked >> 4, stacked & 15
    return ((r < RANK) & (packed == RANK * m + r)).astype(jnp.bfloat16)


def pack_kernel(x_ref, err_hbm, act_hbm, half_ref, runs, err_ref, act_ref, sems):
    ew, aw = err_ref.shape[2] // SEGS, act_ref.shape[2] // SEGS
    n = SEGS // 2
    copies = [
        pltpu.make_async_copy(err_hbm, err_ref, sems.at[0]),
        pltpu.make_async_copy(act_hbm, act_ref, sems.at[1]),
    ]
    for copy in copies:
        copy.start()
    runs[...] = jnp.zeros_like(runs)
    for copy in copies:
        copy.wait()
    for s in range(SEGS):
        runs[s // n, s % n * ROWS : s % n * ROWS + RANK, :ew] = err_ref[0, :, s * ew : (s + 1) * ew]
        runs[s // n, s % n * ROWS : s % n * ROWS + RANK, ew:] = act_ref[0, :, s * aw : (s + 1) * aw]
    pick = picks((half_ref.shape[0], n * ROWS), 1)
    half = jnp.dot(pick, runs[x_ref[0]], preferred_element_type=jnp.float32)
    half_ref[...] = half.astype(jnp.bfloat16)


def pack(x, err, act):
    width = (err.shape[2] + act.shape[2]) // SEGS
    n = SEGS // 2
    vmem, hbm = pl.BlockSpec(memory_space=pltpu.VMEM), pl.BlockSpec(memory_space=pltpu.HBM)
    return pl.pallas_call(
        pack_kernel,
        out_shape=(
            jax.ShapeDtypeStruct((n * RANK, width), jnp.bfloat16),
            jax.ShapeDtypeStruct((2, n * ROWS, width), jnp.bfloat16),
        ),
        in_specs=[pl.BlockSpec(memory_space=pltpu.SMEM), hbm, hbm],
        out_specs=(vmem, vmem),
        scratch_shapes=[
            pltpu.VMEM(err.shape, err.dtype),
            pltpu.VMEM(act.shape, act.dtype),
            pltpu.SemaphoreType.DMA((2,)),
        ],
        compiler_params=pltpu.CompilerParams(vmem_limit_bytes=LIMIT),
        name="pack",
    )(x, err, act)


def again_kernel(x_ref, runs, half_ref, rest_ref):
    n = SEGS // 2
    pick = picks((half_ref.shape[0], n * ROWS), 1)
    for h, out_ref in ((x_ref[0], half_ref), (1 - x_ref[0], rest_ref)):
        half = jnp.dot(pick, runs[h], preferred_element_type=jnp.float32)
        out_ref[...] = half.astype(jnp.bfloat16)


def pack_again(x, runs):
    vmem = pl.BlockSpec(memory_space=pltpu.VMEM)
    out = jax.ShapeDtypeStruct((SEGS // 2 * RANK, runs.shape[2]), jnp.bfloat16)
    return pl.pallas_call(
        again_kernel,
        out_shape=(out, out),
        in_specs=[pl.BlockSpec(memory_space=pltpu.SMEM), vmem],
        out_specs=(vmem, vmem),
        compiler_params=pltpu.CompilerParams(vmem_limit_bytes=LIMIT),
        cost_estimate=weight(PACK),
        name="pack_again",
    )(x, runs)


def weight(us):
    return pl.CostEstimate(flops=int(us * 1e9), bytes_accessed=int(us * 3e6), transcendentals=0)


def unpack(piece, out_ref, at, ew):
    n = SEGS // 2
    aw = piece.shape[1] - ew
    pick = picks((n * ROWS, piece.shape[0]), 0)
    runs = jnp.dot(pick, piece[...], preferred_element_type=jnp.float32).astype(jnp.bfloat16)
    for s in range(n):
        run = runs[s * ROWS : (s + 1) * ROWS]
        out_ref[at : at + ROWS, s * ew : (s + 1) * ew] = run[:, :ew]
        out_ref[at : at + ROWS, n * ew + s * aw : n * ew + (s + 1) * aw] = run[:, ew:]


def gate_kernel(*refs):
    pass


def gate(*arrays):
    hbm = pl.BlockSpec(memory_space=pl.ANY)
    return pl.pallas_call(
        gate_kernel,
        out_shape=tuple(jax.ShapeDtypeStruct(a.shape, a.dtype) for a in arrays),
        in_specs=[hbm] * len(arrays),
        out_specs=(hbm,) * len(arrays),
        input_output_aliases={i: i for i in range(len(arrays))},
        compiler_params=pltpu.CompilerParams(vmem_limit_bytes=1 << 20),
        cost_estimate=weight(TICK),
        name="gate",
    )(*arrays)


def fetch(half, tokens, buffers, sems):
    jobs = []
    for j, buf in enumerate(buffers):
        width, side = buf.shape[1], j % 2
        start = side * buffers[0].shape[1]
        cut = width // CUTS[side]
        for i in range(CUTS[side]):
            at = pl.ds(pl.multiple_of(half * width + i * cut, cut), cut)
            copy = pltpu.make_async_copy(
                tokens[j].at[:, at], buf.at[:, pl.ds(i * cut, cut)], sems.at[len(jobs)]
            )
            copy.start()
            jobs.append((copy, j, i * cut, start + i * cut, cut))
    return jobs


def project(rows, jobs, buffers):
    sums = [None] * 4
    for copy, j, first, start, cut in jobs:
        copy.wait()
        term = lax.dot_general(
            rows[:, start : start + cut], buffers[j][:, first : first + cut], NT,
            preferred_element_type=jnp.float32,
        )
        sums[j] = term if sums[j] is None else sums[j] + term
    return sums


def half_scratch(tokens):
    return [pltpu.VMEM((a.shape[0], a.shape[1] // 2), a.dtype) for a in tokens] + [
        pltpu.SemaphoreType.DMA((len(tokens) // 2 * sum(CUTS),))
    ]


def unpack_kernel(now, later, ew, *refs):
    pieces, (now_ref, later_ref) = refs[:-2], refs[-2:]
    for out_ref, parts in ((now_ref, now), (later_ref, later)):
        for i, p in enumerate(parts):
            unpack(pieces[p], out_ref, i * ROWS, ew)


def unpacked(pieces, now, later, ew):
    vmem = pl.BlockSpec(memory_space=pltpu.VMEM)
    width = SEGS // 2 * pieces[0].shape[1]
    return pl.pallas_call(
        functools.partial(unpack_kernel, now, later, ew),
        out_shape=tuple(
            jax.ShapeDtypeStruct((len(p) * ROWS, width), jnp.bfloat16) for p in (now, later)
        ),
        in_specs=[vmem] * len(pieces),
        out_specs=(vmem, vmem),
        compiler_params=pltpu.CompilerParams(vmem_limit_bytes=LIMIT),
        cost_estimate=weight(TICK),
        name="unpacked",
    )(*pieces)


def first_kernel(now, n_pieces, x_ref, rows_ref, *refs):
    pieces, refs = refs[:n_pieces], refs[n_pieces:]
    tokens, accs, staged = refs[:4], refs[4:8], refs[8:12]
    rows, *buffers, sems, staged_sems = refs[12:]
    jobs = fetch(x_ref[0], tokens, buffers, sems)
    copies = []
    for j, (src, dst) in enumerate(zip(tokens, staged)):
        width = dst.shape[1]
        at = pl.ds(pl.multiple_of((1 - x_ref[0]) * width, width), width)
        copies.append(pltpu.make_async_copy(src.at[:, at], dst, staged_sems.at[j]))
        copies[j].start()
    ew, n = tokens[0].shape[1] // SEGS, rows_ref.shape[0]
    rows[:n] = rows_ref[...]
    for i, p in enumerate(now):
        unpack(pieces[p], rows, n + i * ROWS, ew)
    for acc, v in zip(accs, project(rows, jobs, buffers)):
        acc[...] = v
    for copy in copies:
        copy.wait()


def first_half(x, rows, pieces, now, tokens):
    vmem, hbm = pl.BlockSpec(memory_space=pltpu.VMEM), pl.BlockSpec(memory_space=pltpu.HBM)
    n, width = rows.shape[0] + len(now) * ROWS, rows.shape[1]
    acc = jax.ShapeDtypeStruct((n, tokens[0].shape[0]), jnp.float32)
    return pl.pallas_call(
        functools.partial(first_kernel, now, len(pieces)),
        out_shape=(acc,) * 4
        + tuple(jax.ShapeDtypeStruct((a.shape[0], a.shape[1] // 2), a.dtype) for a in tokens),
        in_specs=[pl.BlockSpec(memory_space=pltpu.SMEM)] + [vmem] * (len(pieces) + 1) + [hbm] * 4,
        out_specs=(vmem,) * 8,
        scratch_shapes=[pltpu.VMEM((n, width), jnp.bfloat16)]
        + half_scratch(tokens)
        + [pltpu.SemaphoreType.DMA((4,))],
        compiler_params=pltpu.CompilerParams(vmem_limit_bytes=LIMIT),
        cost_estimate=weight(12),
        name="first_half",
    )(x, rows, *pieces, *tokens)


def side_sums(rows, tokens):
    sums, start = [], 0
    for t_ref, cuts in zip(tokens, CUTS):
        cut, total = t_ref.shape[1] // cuts, None
        for i in range(cuts):
            term = lax.dot_general(
                rows[:, start : start + cut], t_ref[:, i * cut : (i + 1) * cut], NT,
                preferred_element_type=jnp.float32,
            )
            total = term if total is None else total + term
            start += cut
        sums.append(total)
    return sums


def scores(order, me, sums, accs, out_ref):
    prod = (sums[0] + accs[0][...]) * (sums[1] + accs[1][...])
    out_ref[...] = jnp.zeros_like(out_ref)
    for b, flip in enumerate(order):
        row = jnp.sum(prod[b * ROWS : (b + 1) * ROWS], axis=0, keepdims=True)
        out_ref[pl.ds(jnp.bitwise_xor(me, flip), 1), :] = row


def mate_kernel(order, n_pieces, me_ref, rows_ref, *refs):
    pieces, refs = refs[:n_pieces], refs[n_pieces:]
    tokens, accs, (out_ref, rows) = refs[:2], refs[2:4], refs[4:]
    n = rows_ref.shape[0]
    rows[:n] = rows_ref[...]
    for i, piece in enumerate(pieces):
        unpack(piece, rows, n + i * ROWS, 2 * tokens[0].shape[1] // SEGS)
    scores(order, me_ref[0], side_sums(rows, tokens), accs, out_ref)


def own_kernel(order, me_ref, rows, *refs):
    tokens, accs, out_ref = refs[:2], refs[2:4], refs[4]
    scores(order, me_ref[0], side_sums(rows, tokens), accs, out_ref)


def mate_scores(me, order, rows, pieces, tokens, accs):
    vmem, smem = pl.BlockSpec(memory_space=pltpu.VMEM), pl.BlockSpec(memory_space=pltpu.SMEM)
    return pl.pallas_call(
        functools.partial(mate_kernel, order, len(pieces)),
        out_shape=(
            jax.ShapeDtypeStruct((2 * len(order), tokens[0].shape[0]), jnp.float32),
            jax.ShapeDtypeStruct((len(order) * ROWS, rows.shape[1]), jnp.bfloat16),
        ),
        in_specs=[smem] + [vmem] * (5 + len(pieces)),
        out_specs=(vmem, vmem),
        compiler_params=pltpu.CompilerParams(vmem_limit_bytes=LIMIT),
        cost_estimate=weight(5),
        name="mate_scores",
    )(me, rows, *pieces, *tokens, *accs)


def own_scores(me, order, rows, tokens, accs):
    vmem, smem = pl.BlockSpec(memory_space=pltpu.VMEM), pl.BlockSpec(memory_space=pltpu.SMEM)
    return pl.pallas_call(
        functools.partial(own_kernel, order),
        out_shape=jax.ShapeDtypeStruct((2 * len(order), tokens[0].shape[0]), jnp.float32),
        in_specs=[smem] + [vmem] * 5,
        out_specs=vmem,
        compiler_params=pltpu.CompilerParams(vmem_limit_bytes=LIMIT),
        cost_estimate=weight(30),
        name="own_scores",
    )(me, rows, *tokens, *accs)


def pairs(n_grp, n_blk, flip_grp, flip_blk):
    return [
        (g * n_blk + b, (g ^ flip_grp) * n_blk + (b ^ flip_blk))
        for g in range(n_grp)
        for b in range(n_blk)
    ]


def in_hbm(a):
    return pltpu.with_memory_space_constraint(a, pltpu.HBM)


def permuted(n_grp, n_blk, activations, errors, err_factors, act_factors):
    swap = lambda a, gx, bx: lax.ppermute(a, AXES, pairs(n_grp, n_blk, gx, bx))
    over_x = lambda a: swap(a, 1, 0)
    over_y = lambda a: swap(a, 0, 2)
    over_z = lambda a, k: swap(a, 0, 4 * k)
    over_xy = lambda a: swap(a, 1, 2)
    mate = lambda a: swap(a, 0, 1)
    x = lax.axis_index("grp").astype(jnp.int32).reshape(1)
    me = lax.axis_index("blk").astype(jnp.int32).reshape(1)

    mate_acts, mate_errs = mate(activations), mate(errors)
    half, runs = pack(x, in_hbm(err_factors), in_hbm(act_factors))
    z3 = over_z(half, 3)
    half, rest = pack_again(x, runs)
    y0, z1, y0r = over_y(half), over_z(half, 1), over_y(rest)
    y0, y0r, rest, mate_acts = gate(y0, y0r, rest, mate_acts)
    z2, y3, xa3 = over_z(z3, 1), over_y(z3), over_x(z3)
    y1, y1r = over_z(y0, 1), over_z(y0r, 1)
    z2, y3, xa3, rest, z1 = gate(z2, y3, xa3, rest, z1)
    y2, xa2, xb3 = over_y(z2), over_x(z2), over_y(xa3)
    z1r = over_z(rest, 1)
    mine, others = unpacked(
        (half, y0, z3, z1, y1, z2, y3, rest, y0r, xa3), tuple(range(7)), (7, 8, 9),
        errors.shape[1] // SEGS,
    )
    xb2 = over_x(y2)

    tokens = tuple(in_hbm(a) for a in (errors, activations, mate_errs, mate_acts))
    *accs, e0, a0, e1, a1 = first_half(x, mine, (y2,), (0,), tokens)
    order = (0, 2, 12, 4, 6, 8, 14, 10)
    mates, rows = mate_scores(
        me, order, others, (z1r, y1r, xa2, xb3, xb2), (e1, a1), accs[2:]
    )
    return mate(mates) + own_scores(me, order, rows, (e0, a0), accs[:2])


def solution(mesh):
    in_specs = (
        P(("grp", "blk"), None),
        P(("grp", "blk"), None),
        P("blk", None, None),
        P("blk", None, None),
    )
    out_specs = P(None, ("grp", "blk"))
    n_grp, n_blk = mesh.shape["grp"], mesh.shape["blk"]
    body = gathered
    if (n_grp, n_blk) == (2, 16):
        body = functools.partial(permuted, n_grp, n_blk)
    return jax.shard_map(body, mesh=mesh, in_specs=in_specs, out_specs=out_specs, check_vma=False)
```
